128 devices in a mesh: dp: 16 (over x, z_hi, core), tensor: 8 (over y, z_lo).
Axes of the slice: x: 4, y: 4, z: 4 (z_hi: 2, z_lo: 2; z = z_hi * 2 + z_lo), core: 2. Of those that a mesh axis runs over, the one named last changes fastest.
Arguments:
- inputs: bfloat16 [1024, 12288], P('tensor', 'dp'), may hold values from -11 to 14, as said below
- norm_gain: float32 [12288], P('dp'), may hold values from 0.5 to 1.5
- norm_bias: float32 [12288], P('dp'), may hold values from -3 to 3
- w_up: bfloat16 [12288, 24576], P('dp', 'tensor'), may hold values from -0.0546875 to 0.0546875
- b_up: float32 [24576], P('tensor'), may hold values from -3 to 3
- w_down: bfloat16 [24576, 12288], P('tensor', 'dp'), may hold values from -0.0390625 to 0.0390625
- b_down: float32 [12288], P('dp'), may hold values from -3 to 3
- d_branch: bfloat16 [1024, 12288], P('tensor', 'dp'), may hold values from -6 to 6
Outputs:
- branch: bfloat16 [1024, 12288], P('tensor', 'dp')
- grad_inputs: bfloat16 [1024, 12288], P('tensor', 'dp')
- grad_w_up: bfloat16 [12288, 24576], P('dp', 'tensor')
- grad_b_up: float32 [24576], P('tensor')
- grad_w_down: bfloat16 [24576, 12288], P('tensor', 'dp')
- grad_b_down: float32 [12288], P('dp')
- grad_gain: float32 [12288], P('dp')
- grad_bias: float32 [12288], P('dp')
The draws below stay inside these ranges and needn't reach their ends.
Inputs may be any that keep to these rules, and one draw needn't show every extreme that they name: inputs are finite values of the residual stream.
All inputs are finite; a program needn't handle non-finite values.
Results may differ from the reference program's by a relative error of at most 0.025.
Values may be sent and summed in bfloat16 or wider, within the bound.
A program may use at most 128 MiB of HBM per device.

```python
import jax
import jax.numpy as jnp
from jax import lax

D = 12288
FF = 24576
TOKENS = 1024
N_DP = 16
N_TENSOR = 8


def draw_inputs(key, part):
    key = jax.random.fold_in(key, 11)
    noise_key, amp_key = jax.random.split(key)
    feature = jnp.arange(D, dtype=jnp.float32) / D
    noise = jnp.clip(jax.random.normal(noise_key, (TOKENS, D), jnp.float32), -6.0, 6.0)
    scales = 0.6 + 1.2 * feature
    amplitude = jax.random.uniform(amp_key, (TOKENS, 1), jnp.float32, 0.5, 1.5)
    offset = amplitude * (0.5 + 1.5 * feature)
    return (noise * scales + offset).astype(jnp.bfloat16)


def block_levels(key, shape, shards, least, largest):
    gain, own = 1.0, jax.random.fold_in(key, 6)
    for position, shards_of in shards:
        draws = jnp.exp(jax.random.uniform(jax.random.fold_in(own, position), (shards_of,), jnp.float32, least / len(shards), largest / len(shards)))
        gain = gain * jnp.repeat(draws, shape[position] // shards_of).reshape([-1 if axis == position else 1 for axis in range(len(shape))])
    return gain


def scatter_about(key, dims, scale, reach, pieces=(), kind=jnp.bfloat16):
    entries = scale * jax.random.normal(key, dims, jnp.float32)
    if pieces:
        entries = entries * block_levels(key, dims, pieces, -0.22, 0.18)
    return jnp.clip(entries, -reach, reach).astype(kind)


def setup_inputs(seed: int = 0) -> dict:
    arg_keys = jax.random.split(jax.random.key(seed), 9)
    return {
        "inputs": draw_inputs(jax.random.fold_in(arg_keys[8], 71), 0),
        "norm_gain": jnp.clip(1.0 + 0.1 * jax.random.normal(arg_keys[1], (D,), jnp.float32), 0.5, 1.5),
        "norm_bias": scatter_about(arg_keys[2], (D,), 0.5, 3.0, ((0, 16),), jnp.float32),
        "w_up": scatter_about(arg_keys[3], (D, FF), D ** -0.5, 0.0546875, ((0, 16), (1, 8))),
        "b_up": scatter_about(arg_keys[4], (FF,), 0.5, 3.0, ((0, 8),), jnp.float32),
        "w_down": scatter_about(arg_keys[5], (FF, D), FF ** -0.5, 0.0390625, ((0, 8), (1, 16))),
        "b_down": scatter_about(arg_keys[6], (D,), 0.5, 3.0, ((0, 16),), jnp.float32),
        "d_branch": scatter_about(arg_keys[7], (TOKENS, D), 1.0, 6.0, ((0, 8), (1, 16))),
    }


def block_sum(left, right, count_blocks):
    row_count = left.shape[0]
    inner = left.shape[1]
    columns = right.shape[1]
    block_size = inner // count_blocks
    lefts = left.reshape(row_count, count_blocks, block_size).transpose(1, 0, 2)
    rights = right.reshape(count_blocks, block_size, columns)

    def advance(total, pair):
        term = jnp.dot(pair[0], pair[1], preferred_element_type=jnp.float32).astype(jnp.bfloat16)
        term = lax.optimization_barrier(term)
        return (total + term.astype(jnp.float32), None)
    total, _ = lax.scan(advance, jnp.zeros((row_count, columns), jnp.float32), (lefts, rights))
    return total

def gelu_tanh(value):
    return jax.nn.gelu(value, approximate=True)

def reference(inputs, norm_gain, norm_bias, w_up, b_up, w_down, b_down, d_branch):
    widened = inputs.astype(jnp.float32)
    centre = lax.optimization_barrier(jnp.mean(widened, axis=1, keepdims=True))
    centred = widened - centre
    spread = lax.optimization_barrier(jnp.mean(centred * centred, axis=1, keepdims=True))
    inverse = lax.rsqrt(spread + 1e-05)
    standard = centred * inverse
    normed = (standard * norm_gain + norm_bias).astype(jnp.bfloat16)
    hidden_pre = block_sum(normed, w_up, N_DP) + b_up
    act = gelu_tanh(hidden_pre).astype(jnp.bfloat16)
    branch = (block_sum(act, w_down, N_TENSOR) + b_down).astype(jnp.bfloat16)
    grad_act = block_sum(d_branch, w_down.T, N_DP)
    _, pullback = jax.vjp(gelu_tanh, hidden_pre)
    grad_hidden = pullback(grad_act)[0].astype(jnp.bfloat16)
    grad_w_down = jnp.dot(act.T, d_branch, preferred_element_type=jnp.float32).astype(jnp.bfloat16)
    grad_b_down = lax.optimization_barrier(jnp.sum(d_branch.astype(jnp.float32), axis=0))
    grad_w_up = jnp.dot(normed.T, grad_hidden, preferred_element_type=jnp.float32).astype(jnp.bfloat16)
    grad_b_up = lax.optimization_barrier(jnp.sum(grad_hidden.astype(jnp.float32), axis=0))
    grad_normed = block_sum(grad_hidden, w_up.T, N_TENSOR)
    grad_gain = lax.optimization_barrier(jnp.sum(grad_normed * standard, axis=0))
    grad_bias = lax.optimization_barrier(jnp.sum(grad_normed, axis=0))
    scaled = grad_normed * norm_gain
    grad_inputs = inverse * (scaled - lax.optimization_barrier(jnp.mean(scaled, axis=1, keepdims=True)) - standard * lax.optimization_barrier(jnp.mean(scaled * standard, axis=1, keepdims=True)))
    return (branch, grad_inputs.astype(jnp.bfloat16), grad_w_up, grad_b_up, grad_w_down, grad_b_down, grad_gain, grad_bias)
```

```python
import functools

import jax
import jax.numpy as jnp
from jax import lax
from jax.experimental import pallas as pl
from jax.experimental.pallas import tpu as pltpu
from jax.sharding import PartitionSpec as P

MESH = pl.DeviceIdType.MESH
F32, BF16 = jnp.float32, jnp.bfloat16

D = 12288
N_X, N_Y = 4, 4
WIDE = 768
HALF = 1536
CHUNKS = 4
ROWS = 256
OWN = 32
TILE = 512
K0 = 0.7978845608028654
K1 = 0.044715


def transposed_dot(left, right):
    return lax.dot_general(left, right, (((1,), (1,)), ((), ())), preferred_element_type=F32)


def columns_to_rows(first, second):
    lane = lax.broadcasted_iota(jnp.int32, (128, 128), 1)
    return jnp.where(lane == 0, first, jnp.where(lane == 1, second, 0.0)).T[0:8, :]


def rows_to_columns(first, second):
    row = lax.broadcasted_iota(jnp.int32, (128, 128), 0)
    both = jnp.where(row == 0, first, jnp.where(row == 1, second, 0.0)).T
    return both[:, 0:1], both[:, 1:2]


def kernel(
    x_ref, gain_ref, bias_ref, b_up_ref, b_down_ref, d_ref, w_up_hbm, w_down_hbm,
    branch_ref, grad_in_ref, grad_gain_ref, grad_bias_ref, act_hbm, gh_hbm, nrm_hbm, dbr_hbm,
    w_up, w_down, dbr, nrm, part, core_in, x1_in, x2_in, z_in, full, t_out, t_in,
    standard, grad_normed, stats, back_stats, gb,
    load_sem, store_sem, t_send, t_recv, core_send, core_recv, x1_send, x1_recv, x2_send, x2_recv,
    z_send, z_recv, gz_send, gz_recv, gx_send, gx_recv, gf_send, gf_recv, gc_send, gc_recv,
    ts_send, ts_recv, st_send, st_recv, bs_send, bs_recv, gb_send, gb_recv,
):
    dp, tensor = lax.axis_index("dp"), lax.axis_index("tensor")
    xi, zh, core = dp // 4, (dp // 2) % 2, dp % 2
    yi, zl = tensor // 2, tensor % 2
    right = (((xi + 1) % 4) * 4 + zh * 2 + core, tensor)
    left = (((xi + 3) % 4) * 4 + zh * 2 + core, tensor)
    across = (xi * 4 + (1 - zh) * 2 + core, tensor)
    sibling = (xi * 4 + zh * 2 + (1 - core), tensor)
    x_right, x_left, x_far = (xi + 1) % 4, (xi + 3) % 4, (xi + 2) % 4

    t_to = []
    for dy in range(4):
        for dz in range(2):
            if dy or dz:
                t_to.append((dp, ((yi + dy) % 4) * 2 + (1 - zl if dz else zl)))
    d_to = []
    for dx in range(4):
        for mz in range(2):
            for mc in range(2):
                if dx or mz or mc:
                    d_to.append((((xi + dx) % 4) * 4 + (1 - zh if mz else zh) * 2 + (1 - core if mc else core), tensor))

    load_down = pltpu.make_async_copy(w_down_hbm, w_down, load_sem.at[0])
    load_down.start()
    load_up = [pltpu.make_async_copy(w_up_hbm.at[:, pl.ds(h * HALF, HALF)], w_up.at[h], load_sem.at[1 + h]) for h in range(2)]
    for copy in load_up:
        copy.start()

    barrier = pltpu.get_barrier_semaphore()
    for device in t_to + d_to:
        pl.semaphore_signal(barrier, inc=1, device_id=device, device_id_type=MESH)

    for c in range(CHUNKS):
        dbr[c, pl.ds(tensor * OWN, OWN), :] = d_ref[c * OWN : (c + 1) * OWN, :]
    pl.semaphore_wait(barrier, len(t_to) + len(d_to))

    sent = []

    def send(source, target, send_sem, recv_sem, device):
        copy = pltpu.make_async_remote_copy(
            src_ref=source, dst_ref=target, send_sem=send_sem, recv_sem=recv_sem, device_id=device, device_id_type=MESH
        )
        copy.start()
        sent.append(copy)
        return copy

    def gather_tokens(array, which):
        made = []
        for c in range(CHUNKS):
            place = array.at[c, pl.ds(tensor * OWN, OWN)]
            made.append([send(place, place, t_send.at[which, c, s], t_recv.at[which, c, s], device) for s, device in enumerate(t_to)])
        return made

    dbr_copies = gather_tokens(dbr, 0)

    widened = x_ref[...].astype(F32)
    total = jnp.sum(widened, axis=1, keepdims=True)
    off = widened - total / WIDE
    stats[0] = columns_to_rows(total, jnp.sum(off * off, axis=1, keepdims=True))
    stat_copies = [send(stats.at[0], stats.at[s + 1], st_send.at[s], st_recv.at[s], device) for s, device in enumerate(d_to)]

    def normalise():
        for copy in stat_copies:
            copy.wait_recv()
        sums = [stats[s, 0:1, :] for s in range(16)]
        mean = functools.reduce(jnp.add, sums) / D
        spread = jnp.zeros_like(mean)
        for s in range(16):
            apart = sums[s] / WIDE - mean
            spread = spread + (stats[s, 1:2, :] + WIDE * (apart * apart))
        inverse_row = lax.rsqrt(spread / D + 1e-05)
        mean, inverse = rows_to_columns(mean, inverse_row)
        for c in range(CHUNKS):
            rows = slice(c * OWN, (c + 1) * OWN)
            std = (x_ref[rows, :].astype(F32) - mean[rows]) * inverse[rows]
            standard[rows, :] = std
            nrm[c, pl.ds(tensor * OWN, OWN), :] = (std * gain_ref[...] + bias_ref[...]).astype(BF16)
        return inverse, gather_tokens(nrm, 1)

    core_copies, x1_copies, x2_copies, z_copies = {}, {}, {}, {}

    def multiply(u):
        c, k = u // 2, u % 2
        source = nrm if k else dbr
        for s in (nrm_copies if k else dbr_copies)[c]:
            s.wait_recv()
        for step in range(2):
            half = (1 - core) if step == 0 else core

            def tile(j, _):
                at = pl.multiple_of(j * TILE, TILE)
                if k:
                    value = jnp.dot(source[c], w_up[half, :, pl.ds(at, TILE)], preferred_element_type=F32)
                else:
                    value = transposed_dot(source[c], w_down[half, pl.ds(at, TILE), :])
                part[u, half, :, pl.ds(at, TILE)] = value.astype(BF16)
                return 0

            lax.fori_loop(0, HALF // TILE, tile, 0)
            if step == 0:
                core_copies[u] = send(part.at[u, half], core_in.at[u], core_send.at[u], core_recv.at[u], sibling)

    def add_core(u):
        core_copies[u].wait_recv()

        def block(i, _):
            rows = pl.ds(pl.multiple_of(i * 16, 16), 16)
            part[u, core, rows, :] = (part[u, core, rows, :].astype(F32) + core_in[u, rows, :].astype(F32)).astype(BF16)
            return 0

        lax.fori_loop(0, ROWS // 16, block, 0)
        x1_copies[u] = [
            send(part.at[u, core, pl.ds(x_far * 64, 32)], x1_in.at[u, 0], x1_send.at[u, 0], x1_recv.at[u, 0], right),
            send(part.at[u, core, pl.ds(x_far * 64 + 32, 32)], x1_in.at[u, 1], x1_send.at[u, 1], x1_recv.at[u, 1], left),
        ]

    def add_x1(u):
        x2_copies[u] = []
        for side, (piece, device) in enumerate(((x_right, right), (x_left, left))):
            x1_copies[u][side].wait_recv()
            for i in range(2):
                rows = pl.ds(pl.multiple_of(piece * 64 + side * 32 + i * 16, 16), 16)
                there = x1_in[u, side, i * 16 : (i + 1) * 16, :]
                part[u, core, rows, :] = (part[u, core, rows, :].astype(F32) + there.astype(F32)).astype(BF16)
            x2_copies[u].append(
                send(part.at[u, core, pl.ds(piece * 64, 64)], x2_in.at[u, side], x2_send.at[u, side], x2_recv.at[u, side], device)
            )

    def add_x2(u):
        for copy in x2_copies[u]:
            copy.wait_recv()
        for sub in (1 - zh, zh):
            for i in range(2):
                at = pl.multiple_of(sub * 32 + i * 16, 16)
                rows = pl.ds(pl.multiple_of(xi * 64 + at, 16), 16)
                there = x2_in[u, 0, pl.ds(at, 16), :].astype(F32) + x2_in[u, 1, pl.ds(at, 16), :].astype(F32)
                part[u, core, rows, :] = (part[u, core, rows, :].astype(F32) + there).astype(BF16)
            if sub is not zh:
                place = part.at[u, core, pl.ds(xi * 64 + (1 - zh) * 32, 32)]
                z_copies[u] = send(place, z_in.at[u], z_send.at[u], z_recv.at[u], across)

    gz, gx, gf, gc = {}, {}, {}, {}
    mine = xi * 64 + zh * 32

    def activate(c):
        z_copies[2 * c].wait_recv()
        z_copies[2 * c + 1].wait_recv()
        bias = b_up_ref[core]
        for i in range(2):
            rows = pl.ds(pl.multiple_of(mine + i * 16, 16), 16)
            here = slice(i * 16, (i + 1) * 16)
            ga = part[2 * c, core, rows, :].astype(F32) + z_in[2 * c, here, :].astype(F32)
            h = part[2 * c + 1, core, rows, :].astype(F32) + z_in[2 * c + 1, here, :].astype(F32) + bias
            square = h * h
            t = jnp.tanh(K0 * (h + K1 * (square * h)))
            full[0, c, core, rows, :] = (0.5 * h * (1.0 + t)).astype(BF16)
            slope = 0.5 * (1.0 + t) + 0.5 * h * (1.0 - t * t) * (K0 * (1.0 + 3.0 * K1 * square))
            full[1, c, core, rows, :] = (ga * slope).astype(BF16)
        for k in range(2):
            place = full.at[k, c, core, pl.ds(mine, 32)]
            gz[k, c] = send(place, place, gz_send.at[k, c], gz_recv.at[k, c], across)

    def to_sibling(k, c, slot, piece):
        place = full.at[k, c, core, pl.ds(piece * 64, 64)]
        gc[k, c, slot] = send(place, place, gc_send.at[k, c, slot], gc_recv.at[k, c, slot], sibling)

    def gather_x(c):
        for k in range(2):
            gz[k, c].wait_recv()
            place = full.at[k, c, core, pl.ds(xi * 64, 64)]
            for side, device in enumerate((right, left)):
                gx[k, c, side] = send(place, place, gx_send.at[k, c, side], gx_recv.at[k, c, side], device)
            to_sibling(k, c, 0, xi)

    def forward_x(c):
        for k in range(2):
            for side, (piece, device) in enumerate(((x_left, right), (x_right, left))):
                gx[k, c, side].wait_recv()
                place = full.at[k, c, core, pl.ds(piece * 64 + side * 32, 32)]
                gf[k, c, side] = send(place, place, gf_send.at[k, c, side], gf_recv.at[k, c, side], device)
                to_sibling(k, c, 1 + side, piece)

    def last_x(c):
        for k in range(2):
            for side in range(2):
                gf[k, c, side].wait_recv()
            to_sibling(k, c, 3, x_far)

    stores, ts = [], {}

    def store(source, target, index):
        copy = pltpu.make_async_copy(source, target, store_sem.at[index])
        copy.start()
        stores.append(copy)

    def multiply_back(c):
        for k in range(2):
            for slot in range(4):
                gc[k, c, slot].wait_recv()

            def tile(j, _):
                at = pl.multiple_of(j * 256, 256)
                if k:
                    value = transposed_dot(full[1, c, 0], w_up[0, pl.ds(at, 256), :])
                    value += transposed_dot(full[1, c, 1], w_up[1, pl.ds(at, 256), :])
                else:
                    value = jnp.dot(full[0, c, 0], w_down[0, :, pl.ds(at, 256)], preferred_element_type=F32)
                    value += jnp.dot(full[0, c, 1], w_down[1, :, pl.ds(at, 256)], preferred_element_type=F32)
                t_out[k, c, :, pl.ds(at, 256)] = value.astype(BF16)
                return 0

            lax.fori_loop(0, WIDE // 256, tile, 0)
            for s, device in enumerate(t_to):
                place = t_out.at[k, c, pl.ds(device[1] * OWN, OWN)]
                ts[k, c, s] = send(place, t_in.at[k, c, s], ts_send.at[k, c, s], ts_recv.at[k, c, s], device)
            for half in range(2):
                target = (gh_hbm if k else act_hbm).at[pl.ds(c * ROWS, ROWS), pl.ds(half * HALF, HALF)]
                store(full.at[k, c, half], target, (k * CHUNKS + c) * 2 + half)

    def finish_tokens(c):
        for k in range(2):
            for s in range(7):
                ts[k, c, s].wait_recv()
            value = t_out[k, c, pl.ds(pl.multiple_of(tensor * OWN, OWN), OWN), :].astype(F32)
            for s in range(7):
                value = value + t_in[k, c, s].astype(F32)
            rows = slice(c * OWN, (c + 1) * OWN)
            if k:
                grad_normed[rows, :] = value
            else:
                branch_ref[rows, :] = (value + b_down_ref[...]).astype(BF16)

    units = 2 * CHUNKS
    load_down.wait()
    inverse = None
    for slot in range(-1, units + 8):
        if 0 <= slot + 1 < units:
            if slot + 1 == 1:
                inverse, nrm_copies = normalise()
                for copy in load_up:
                    copy.wait()
            multiply(slot + 1)
            add_core(slot + 1)
        if 0 <= slot < units:
            add_x1(slot)
        if 0 <= slot - 1 < units:
            add_x2(slot - 1)
        for offset, step in ((3, activate), (4, gather_x), (5, forward_x), (6, last_x), (7, multiply_back), (8, finish_tokens)):
            c, rest = divmod(slot - offset, 2)
            if 0 <= c < CHUNKS and rest == 0:
                step(c)

    for c in range(CHUNKS):
        store(dbr.at[c], dbr_hbm.at[pl.ds(c * ROWS, ROWS)], 16 + c)
        store(nrm.at[c], nrm_hbm.at[pl.ds(c * ROWS, ROWS)], 20 + c)

    gn = grad_normed[...]
    std = standard[...]
    scaled = gn * gain_ref[...]
    back_stats[0] = columns_to_rows(
        jnp.sum(scaled, axis=1, keepdims=True), jnp.sum(scaled * std, axis=1, keepdims=True)
    )
    back_copies = [
        send(back_stats.at[0], back_stats.at[s + 1], bs_send.at[s], bs_recv.at[s], device) for s, device in enumerate(d_to)
    ]
    gb[0, 0:1, :] = jnp.sum(gn * std, axis=0, keepdims=True)
    gb[0, 1:2, :] = jnp.sum(gn, axis=0, keepdims=True)
    gb[0, 2:8, :] = jnp.zeros((6, WIDE), F32)
    gb_copies = [send(gb.at[0], gb.at[s + 1], gb_send.at[s], gb_recv.at[s], device) for s, device in enumerate(t_to)]
    for copy in back_copies:
        copy.wait_recv()
    first = functools.reduce(jnp.add, [back_stats[s, 0:1, :] for s in range(16)]) / D
    second = functools.reduce(jnp.add, [back_stats[s, 1:2, :] for s in range(16)]) / D
    first, second = rows_to_columns(first, second)
    grad_in_ref[...] = (inverse * (scaled - first - std * second)).astype(BF16)
    for copy in gb_copies:
        copy.wait_recv()
    both = functools.reduce(jnp.add, [gb[s] for s in range(8)])
    grad_gain_ref[...] = both[0:1, :]
    grad_bias_ref[...] = both[1:2, :]

    for copy in stores:
        copy.wait()
    for copy in sent:
        copy.wait_send()


def on_device(inputs, norm_gain, norm_bias, w_up, b_up, w_down, b_down, d_branch):
    vmem = pl.BlockSpec(memory_space=pltpu.VMEM)
    hbm = pl.BlockSpec(memory_space=pl.ANY)
    units = 2 * CHUNKS
    dma = pltpu.SemaphoreType.DMA
    shape = jax.ShapeDtypeStruct
    branch, grad_inputs, grad_gain, grad_bias, act, gh, nrm, dbr = pl.pallas_call(
        kernel,
        out_shape=(
            shape((128, WIDE), BF16), shape((128, WIDE), BF16), shape((1, WIDE), F32), shape((1, WIDE), F32),
            shape((1024, 2 * HALF), BF16), shape((1024, 2 * HALF), BF16), shape((1024, WIDE), BF16), shape((1024, WIDE), BF16),
        ),
        in_specs=[vmem] * 6 + [hbm] * 2,
        out_specs=(vmem,) * 4 + (hbm,) * 4,
        scratch_shapes=[
            pltpu.VMEM((2, WIDE, HALF), BF16),
            pltpu.VMEM((2, HALF, WIDE), BF16),
            pltpu.VMEM((CHUNKS, ROWS, WIDE), BF16),
            pltpu.VMEM((CHUNKS, ROWS, WIDE), BF16),
            pltpu.VMEM((units, 2, ROWS, HALF), BF16),
            pltpu.VMEM((units, ROWS, HALF), BF16),
            pltpu.VMEM((units, 2, 32, HALF), BF16),
            pltpu.VMEM((units, 2, 64, HALF), BF16),
            pltpu.VMEM((units, 32, HALF), BF16),
            pltpu.VMEM((2, CHUNKS, 2, ROWS, HALF), BF16),
            pltpu.VMEM((2, CHUNKS, ROWS, WIDE), BF16),
            pltpu.VMEM((2, CHUNKS, 7, OWN, WIDE), BF16),
            pltpu.VMEM((128, WIDE), F32),
            pltpu.VMEM((128, WIDE), F32),
            pltpu.VMEM((16, 8, 128), F32),
            pltpu.VMEM((16, 8, 128), F32),
            pltpu.VMEM((8, 8, WIDE), F32),
            dma((3,)), dma((24,)),
            dma((2, CHUNKS, 7)), dma((2, CHUNKS, 7)),
            dma((units,)), dma((units,)),
            dma((units, 2)), dma((units, 2)),
            dma((units, 2)), dma((units, 2)),
            dma((units,)), dma((units,)),
            dma((2, CHUNKS)), dma((2, CHUNKS)),
            dma((2, CHUNKS, 2)), dma((2, CHUNKS, 2)),
            dma((2, CHUNKS, 2)), dma((2, CHUNKS, 2)),
            dma((2, CHUNKS, 4)), dma((2, CHUNKS, 4)),
            dma((2, CHUNKS, 7)), dma((2, CHUNKS, 7)),
            dma((15,)), dma((15,)), dma((15,)), dma((15,)), dma((7,)), dma((7,)),
        ],
        compiler_params=pltpu.CompilerParams(collective_id=0, has_side_effects=True, vmem_limit_bytes=62 * 2**20),
    )(
        inputs, norm_gain.reshape(1, WIDE), norm_bias.reshape(1, WIDE), b_up.reshape(2, 1, HALF), b_down.reshape(1, WIDE), d_branch,
        w_up, w_down.reshape(2, HALF, WIDE),
    )
    grad_w_down = lax.dot_general(act, dbr, (((0,), (0,)), ((), ())), preferred_element_type=F32).astype(BF16)
    grad_w_up = lax.dot_general(nrm, gh, (((0,), (0,)), ((), ())), preferred_element_type=F32).astype(BF16)
    grad_b_down = jnp.sum(dbr.astype(F32), axis=0)
    grad_b_up = jnp.sum(gh.astype(F32), axis=0)
    return branch, grad_inputs, grad_w_up, grad_b_up, grad_w_down, grad_b_down, grad_gain.reshape(WIDE), grad_bias.reshape(WIDE)


def solution(mesh):
    placed = (
        P("tensor", "dp"), P("dp"), P("dp"), P("dp", "tensor"), P("tensor"), P("tensor", "dp"), P("dp"), P("tensor", "dp"),
    )
    return jax.shard_map(
        on_device,
        mesh=mesh,
        in_specs=placed,
        out_specs=(
            P("tensor", "dp"), P("tensor", "dp"), P("dp", "tensor"), P("tensor"), P("tensor", "dp"), P("dp"), P("dp"), P("dp"),
        ),
        check_vma=False,
    )
```

```python
import functools

import jax
import jax.numpy as jnp
from jax import lax
from jax.experimental import pallas as pl
from jax.experimental.pallas import tpu as pltpu
from jax.sharding import PartitionSpec as P

MESH = pl.DeviceIdType.MESH
F32, BF16 = jnp.float32, jnp.bfloat16

D = 12288
WIDE = 768
HALF = 1536
TOKENS = 1024
STRIP = 512
K0 = 0.7978845608028654
K1 = 0.044715

OWN = (16, 32, 32, 32, 16)
CHUNKS = len(OWN)
OFF = tuple(sum(OWN[:c]) for c in range(CHUNKS))
Z_FIRST = (1,)
T_PAIRS = (1, 2, 3, 4)
R_PAIRS = (0, 1, 2)
Z_ROWS = tuple((4 if c in Z_FIRST else 1) * OWN[c] for c in range(CHUNKS))
Z_OFF = tuple(sum(Z_ROWS[:c]) for c in range(CHUNKS))

ORDER = (
    ("TZ", 0, 1), ("ST", 0, 0), ("TY", 0, 0), ("TZ", 0, 2), ("TZ", 0, 3), ("TY", 0, 1), ("TZ", 0, 4), ("NM", 0, 0),
    ("TZ", 1, 1), ("TY", 1, 0), ("TY", 0, 2), ("M", 0, 0), ("TZ", 1, 2), ("TY", 0, 3), ("TY", 1, 1), ("TZ", 1, 4),
    ("M", 0, 1), ("TY", 1, 2), ("A", 0, 0), ("TY", 0, 4), ("M", 1, 0), ("A", 0, 1), ("A", 1, 0), ("B", 0, 0),
    ("M", 0, 2), ("B", 1, 0), ("M", 0, 3), ("A", 0, 2), ("C", 0, 0), ("TZ", 1, 3), ("A", 0, 3), ("C", 1, 0),
    ("TY", 1, 4), ("B", 0, 1), ("B", 0, 2), ("B", 0, 3), ("TY", 1, 3), ("G", 0, 0), ("M", 1, 1), ("M", 0, 4),
    ("C", 0, 1), ("A", 1, 1), ("M", 1, 2), ("E1", 0, 0), ("A", 1, 2), ("E1", 1, 0), ("M", 1, 3), ("A", 0, 4),
    ("A", 1, 3), ("C", 0, 2), ("B", 1, 1), ("M", 1, 4), ("B", 1, 2), ("A", 1, 4), ("B", 1, 3), ("C", 1, 2),
    ("C", 1, 1), ("B", 1, 4), ("C", 0, 3), ("E2", 1, 0), ("E2", 0, 0), ("C", 1, 3), ("G", 0, 2), ("B", 0, 4),
    ("G", 0, 1), ("E3", 1, 0), ("C", 1, 4), ("F", 1, 0), ("C", 0, 4), ("G", 0, 3), ("E1", 1, 2), ("E3", 0, 0),
    ("E1", 1, 1), ("E1", 0, 1), ("H1", 1, 0), ("E1", 0, 2), ("G", 0, 4), ("F", 0, 0), ("E2", 1, 1), ("E1", 1, 4),
    ("E2", 1, 2), ("E2", 0, 2), ("E2", 0, 1), ("H1", 0, 0), ("H", 1, 0), ("E1", 1, 3), ("E1", 0, 4), ("E1", 0, 3),
    ("E3", 1, 2), ("E3", 1, 1), ("F", 1, 2), ("E3", 0, 2), ("F", 1, 1), ("E2", 1, 3), ("F", 0, 2), ("E2", 1, 4),
    ("E3", 0, 1), ("E2", 0, 4), ("E2", 0, 3), ("F", 0, 1), ("E3", 1, 3), ("H1", 1, 1), ("H", 0, 0), ("E3", 1, 4),
    ("H1", 1, 2), ("F", 1, 3), ("E3", 0, 3), ("F", 1, 4), ("WU", 0, 5), ("F", 0, 3), ("E3", 0, 4), ("WU", 0, 2),
    ("WU", 0, 3), ("F", 0, 4), ("H", 1, 2), ("H1", 0, 1), ("H", 1, 1), ("WD", 0, 2), ("WD", 0, 4), ("H", 1, 4),
    ("H", 1, 3), ("S", 0, 0), ("H1", 0, 2), ("WU", 0, 0), ("WU", 0, 4), ("WD", 0, 3), ("H", 0, 3), ("WD", 0, 0),
    ("H", 0, 2), ("Z", 0, 0), ("H", 0, 1), ("WU", 0, 1), ("H", 0, 4), ("WD", 0, 1), ("WD", 0, 5),
)


def transposed_dot(left, right):
    return lax.dot_general(left, right, (((1,), (1,)), ((), ())), preferred_element_type=F32)


def dot_transposed(left, right):
    return lax.dot_general(left, right, (((0,), (0,)), ((), ())), preferred_element_type=F32)


def columns_to_rows(first, second):
    lane = lax.broadcasted_iota(jnp.int32, (128, 128), 1)
    return jnp.where(lane == 0, first, jnp.where(lane == 1, second, 0.0)).T[0:8, :]


def rows_to_columns(first, second):
    row = lax.broadcasted_iota(jnp.int32, (128, 128), 0)
    both = jnp.where(row == 0, first, jnp.where(row == 1, second, 0.0)).T
    return both[:, 0:1], both[:, 1:2]


def kernel(
    x_ref, gain_ref, bias_ref, b_up_ref, b_down_ref, d_ref, w_up_hbm, w_down_hbm,
    branch_ref, grad_in_ref, grad_gain_ref, grad_bias_ref, grad_b_up_ref, grad_b_down_ref, gw_up_hbm, gw_down_hbm,
    w_up, w_down, dbr, nrm, part, core_in, x1_in, x2_in, z_in, full, t_out, t_in, t_acc,
    standard, grad_normed, inverse_ref, stats, back_stats, gb, gu_tile, gd_tile,
    load_sem, store_sem, t_send, t_recv, tz_send, tz_recv, core_send, core_recv, x1_send, x1_recv, x2_send, x2_recv,
    z_send, z_recv, ga_send, ga_recv, gx_send, gx_recv, gf_send, gf_recv, gc_send, gc_recv,
    ts_send, ts_recv, tr_send, tr_recv, st_send, st_recv, bs_send, bs_recv, gb_send, gb_recv,
):
    dp, tensor = lax.axis_index("dp"), lax.axis_index("tensor")
    xi, zh, core = dp // 4, (dp // 2) % 2, dp % 2
    yi, zl = tensor // 2, tensor % 2
    x_right, x_left, x_far = (xi + 1) % 4, (xi + 3) % 4, (xi + 2) % 4
    right = (x_right * 4 + zh * 2 + core, tensor)
    left = (x_left * 4 + zh * 2 + core, tensor)
    across = (xi * 4 + (1 - zh) * 2 + core, tensor)
    sibling = (xi * 4 + zh * 2 + (1 - core), tensor)
    t_pair = (dp, yi * 2 + (1 - zl))
    y_to = [(dp, ((yi + dy) % 4) * 2 + zl) for dy in (1, 2, 3)]
    t_to = y_to + [t_pair] + [(dp, ((yi + dy) % 4) * 2 + (1 - zl)) for dy in (1, 2, 3)]
    d_to = []
    for dx in range(4):
        for mz in range(2):
            for mc in range(2):
                if dx or mz or mc:
                    d_to.append((((xi + dx) % 4) * 4 + (1 - zh if mz else zh) * 2 + (1 - core if mc else core), tensor))

    loads = [[pltpu.make_async_copy(w_down_hbm, w_down, load_sem.at[0])]]
    loads.append([pltpu.make_async_copy(w_up_hbm.at[:, pl.ds(h * HALF, HALF)], w_up.at[h], load_sem.at[1 + h]) for h in range(2)])
    for copy in loads[0] + loads[1]:
        copy.start()

    barrier = pltpu.get_barrier_semaphore()
    for device in t_to + d_to:
        pl.semaphore_signal(barrier, inc=1, device_id=device, device_id_type=MESH)

    def rows_at(at, count):
        return pl.ds(pl.multiple_of(at, 16), count)

    for c in range(CHUNKS):
        dbr[rows_at(8 * OFF[c] + tensor * OWN[c], OWN[c]), :] = d_ref[OFF[c] : OFF[c] + OWN[c], :]
    pl.semaphore_wait(barrier, len(t_to) + len(d_to))

    sent = []

    def send(source, target, sends, receives, index, device):
        copy = pltpu.make_async_remote_copy(
            src_ref=source, dst_ref=target, send_sem=sends.at[index], recv_sem=receives.at[index],
            device_id=device, device_id_type=MESH,
        )
        copy.start()
        sent.append(copy)
        return copy

    pair_in, token_in, core_arrives, x1_arrives, x2_arrives, z_arrives = {}, {}, {}, {}, {}, {}
    own_in, neighbour_in, far_in, core_full, branch_in, half_in = {}, {}, {}, {}, {}, {}
    small = {}
    tokens = (dbr, nrm)

    def pair_tokens(k, c):
        place = tokens[k].at[rows_at(8 * OFF[c] + tensor * OWN[c], OWN[c])]
        pair_in[k, c] = send(place, place, tz_send, tz_recv, (k, c), t_pair)

    def gather_tokens(k, c):
        if c in T_PAIRS:
            pair_in[k, c].wait_recv()
            place = tokens[k].at[rows_at(8 * OFF[c] + yi * 2 * OWN[c], 2 * OWN[c])]
            to = y_to
        else:
            place = tokens[k].at[rows_at(8 * OFF[c] + tensor * OWN[c], OWN[c])]
            to = t_to
        token_in[k, c] = [send(place, place, t_send, t_recv, (k, c, s), device) for s, device in enumerate(to)]

    def statistics(k, c):
        widened = x_ref[...].astype(F32)
        total = jnp.sum(widened, axis=1, keepdims=True)
        off = widened - total / WIDE
        stats[0] = columns_to_rows(total, jnp.sum(off * off, axis=1, keepdims=True))
        small["forward"] = [send(stats.at[0], stats.at[s + 1], st_send, st_recv, s, device) for s, device in enumerate(d_to)]

    def normalise(k, c):
        for copy in small["forward"]:
            copy.wait_recv()
        sums = [stats[s, 0:1, :] for s in range(16)]
        mean = functools.reduce(jnp.add, sums) / D
        spread = jnp.zeros_like(mean)
        for s in range(16):
            apart = sums[s] / WIDE - mean
            spread = spread + (stats[s, 1:2, :] + WIDE * (apart * apart))
        mean, inverse = rows_to_columns(mean, lax.rsqrt(spread / D + 1e-05))
        inverse_ref[...] = jnp.broadcast_to(inverse, (128, 128))
        gain, bias = gain_ref[...].reshape(1, WIDE), bias_ref[...].reshape(1, WIDE)
        for c in range(CHUNKS):
            rows = slice(OFF[c], OFF[c] + OWN[c])
            std = (x_ref[rows, :].astype(F32) - mean[rows]) * inverse[rows]
            standard[rows, :] = std
            nrm[rows_at(8 * OFF[c] + tensor * OWN[c], OWN[c]), :] = (std * gain + bias).astype(BF16)

    def accumulate(k, c, start, count, others):
        size = 32 if count % 32 == 0 else 16

        def block(i, _):
            at = i * size
            rows = rows_at(8 * OFF[c] + start + at, size)
            value = part[k, core, rows, :].astype(F32)
            for load in others:
                value = value + load(at, size).astype(F32)
            part[k, core, rows, :] = value.astype(BF16)
            return 0

        if count == size:
            block(0, 0)
        else:
            lax.fori_loop(0, count // size, block, 0)

    def multiply(k, c):
        if (k, c) == (k, 0):
            for copy in loads[k]:
                copy.wait()
        for copy in token_in[k, c]:
            copy.wait_recv()
        rows = pl.ds(8 * OFF[c], 8 * OWN[c])
        for half in (1 - core, core):
            if k:
                value = jnp.dot(nrm[rows, :], w_up[half], preferred_element_type=F32)
            else:
                value = transposed_dot(dbr[rows, :], w_down[half])
            part[k, half, rows, :] = value.astype(BF16)
            if (k, c) not in core_arrives:
                core_arrives[k, c] = send(part.at[k, half, rows], core_in.at[k, rows], core_send, core_recv, (k, c), sibling)

    def part_rows(k, c, start, count):
        return part.at[k, core, rows_at(8 * OFF[c] + start, count)]

    def add_core(k, c):
        p = OWN[c]
        core_arrives[k, c].wait_recv()

        def add(start, count):
            accumulate(k, c, start, count, [lambda at, size: core_in[k, rows_at(8 * OFF[c] + start + at, size), :]])

        if c in Z_FIRST:
            add((1 - zh) * 4 * p, 4 * p)
            z_arrives[k, c] = send(
                part_rows(k, c, (1 - zh) * 4 * p, 4 * p), z_in.at[k, pl.ds(Z_OFF[c], 4 * p)], z_send, z_recv, (k, c), across
            )
            add(zh * 4 * p, 4 * p)
        else:
            add(x_far * 2 * p, 2 * p)
            x1_arrives[k, c] = [
                send(
                    part_rows(k, c, x_far * 2 * p + side * p, p), x1_in.at[k, side, pl.ds(OFF[c], p)],
                    x1_send, x1_recv, (k, c, side), device,
                )
                for side, device in enumerate((right, left))
            ]
            for piece in (x_right, x_left, xi):
                add(piece * 2 * p, 2 * p)

    def add_first(k, c):
        p = OWN[c]
        if c in Z_FIRST:
            z_arrives[k, c].wait_recv()

            def add(piece):
                start = piece * p
                accumulate(
                    k, c, zh * 4 * p + start, p, [lambda at, size: z_in[k, rows_at(Z_OFF[c] + start + at, size), :]]
                )

            add(x_far)
            x1_arrives[k, c] = [
                send(
                    part_rows(k, c, zh * 4 * p + x_far * p + side * (p // 2), p // 2),
                    x1_in.at[k, side, pl.ds(OFF[c], p // 2)], x1_send, x1_recv, (k, c, side), device,
                )
                for side, device in enumerate((right, left))
            ]
            for piece in (x_right, x_left, xi):
                add(piece)
        else:
            add_x1(k, c, 2 * p, 0)

    def add_x1(k, c, size, base):
        x2_arrives[k, c] = []
        for side, (piece, device) in enumerate(((x_right, right), (x_left, left))):
            x1_arrives[k, c][side].wait_recv()
            accumulate(
                k, c, base + piece * size + side * (size // 2), size // 2,
                [lambda at, count, side=side: x1_in[k, side, rows_at(OFF[c] + at, count), :]],
            )
            x2_arrives[k, c].append(
                send(
                    part_rows(k, c, base + piece * size, size), x2_in.at[k, side, pl.ds(2 * OFF[c], size)],
                    x2_send, x2_recv, (k, c, side), device,
                )
            )

    def add_second(k, c):
        p = OWN[c]
        if c in Z_FIRST:
            add_x1(k, c, p, zh * 4 * p)
            return
        for copy in x2_arrives[k, c]:
            copy.wait_recv()

        def add(sub):
            start = sub * p
            accumulate(
                k, c, xi * 2 * p + start, p,
                [lambda at, size, side=side: x2_in[k, side, rows_at(2 * OFF[c] + start + at, size), :] for side in range(2)],
            )

        add(1 - zh)
        z_arrives[k, c] = send(
            part_rows(k, c, xi * 2 * p + (1 - zh) * p, p), z_in.at[k, pl.ds(Z_OFF[c], p)], z_send, z_recv, (k, c), across
        )
        add(zh)

    def activate(_, c):
        p = OWN[c]
        if c in Z_FIRST:
            mine = zh * 4 * p + xi * p
            for k in range(2):
                for copy in x2_arrives[k, c]:
                    copy.wait_recv()
        else:
            mine = xi * 2 * p + zh * p
            for k in range(2):
                z_arrives[k, c].wait_recv()
        bias = b_up_ref[pl.ds(pl.multiple_of(core * HALF, HALF), HALF)].reshape(1, HALF)

        def total(k, at):
            value = part[k, core, rows_at(8 * OFF[c] + mine + at, 16), :].astype(F32)
            if c in Z_FIRST:
                for side in range(2):
                    value = value + x2_in[k, side, pl.ds(2 * OFF[c] + at, 16), :].astype(F32)
                return value
            return value + z_in[k, pl.ds(Z_OFF[c] + at, 16), :].astype(F32)

        for at in range(0, p, 16):
            rows = rows_at(8 * OFF[c] + mine + at, 16)
            h = total(1, at) + bias
            square = h * h
            t = jnp.tanh(K0 * (h + K1 * (square * h)))
            full[0, core, rows, :] = (0.5 * h * (1.0 + t)).astype(BF16)
            slope = 0.5 * (1.0 + t) + 0.5 * h * (1.0 - t * t) * (K0 * (1.0 + 3.0 * K1 * square))
            full[1, core, rows, :] = (total(0, at) * slope).astype(BF16)
        for k in (1, 0):
            place = full.at[k, core, rows_at(8 * OFF[c] + mine, p)]
            to = (right, left) if c in Z_FIRST else (across,)
            own_in[k, c] = [send(place, place, ga_send, ga_recv, (k, c, s), device) for s, device in enumerate(to)]

    def full_rows(k, c, start, count):
        return full.at[k, core, rows_at(8 * OFF[c] + start, count)]

    def to_sibling(k, c, start, count):
        arrivals = core_full.setdefault((k, c), [])
        place = full_rows(k, c, start, count)
        arrivals.append(send(place, place, gc_send, gc_recv, (k, c, len(arrivals)), sibling))

    def forward(k, c, arrivals, size, base):
        made = []
        for side, (piece, device) in enumerate(((x_left, right), (x_right, left))):
            arrivals[side].wait_recv()
            place = full_rows(k, c, base + piece * size + side * (size // 2), size // 2)
            made.append(send(place, place, gf_send, gf_recv, (k, c, side), device))
        return made

    def gather_first(k, c):
        p = OWN[c]
        if c in Z_FIRST:
            far_in[k, c] = forward(k, c, own_in[k, c], p, zh * 4 * p)
        else:
            own_in[k, c][0].wait_recv()
            place = full_rows(k, c, xi * 2 * p, 2 * p)
            neighbour_in[k, c] = [
                send(place, place, gx_send, gx_recv, (k, c, side), device) for side, device in enumerate((right, left))
            ]
            to_sibling(k, c, xi * 2 * p, 2 * p)

    def gather_second(k, c):
        p = OWN[c]
        if c in Z_FIRST:
            for copy in far_in[k, c]:
                copy.wait_recv()
            place = full_rows(k, c, zh * 4 * p, 4 * p)
            neighbour_in[k, c] = [send(place, place, gx_send, gx_recv, (k, c, 0), across)]
            to_sibling(k, c, zh * 4 * p, 4 * p)
        else:
            far_in[k, c] = forward(k, c, neighbour_in[k, c], 2 * p, 0)
            for piece in (x_left, x_right):
                to_sibling(k, c, piece * 2 * p, 2 * p)

    def gather_third(k, c):
        p = OWN[c]
        if c in Z_FIRST:
            neighbour_in[k, c][0].wait_recv()
            to_sibling(k, c, (1 - zh) * 4 * p, 4 * p)
        else:
            for copy in far_in[k, c]:
                copy.wait_recv()
            to_sibling(k, c, x_far * 2 * p, 2 * p)

    def multiply_back(k, c):
        p = OWN[c]
        for copy in core_full[k, c]:
            copy.wait_recv()
        rows = pl.ds(8 * OFF[c], 8 * p)
        if k:
            value = transposed_dot(full[1, 0, rows, :], w_up[0]) + transposed_dot(full[1, 1, rows, :], w_up[1])
        else:
            value = jnp.dot(full[0, 0, rows, :], w_down[0], preferred_element_type=F32)
            value += jnp.dot(full[0, 1, rows, :], w_down[1], preferred_element_type=F32)
        t_out[k, rows, :] = value.astype(BF16)
        branch_in[k, c] = []
        if c in R_PAIRS:
            for s, device in enumerate(y_to):
                place = t_out.at[k, rows_at(8 * OFF[c] + (device[1] // 2) * 2 * p, 2 * p)]
                target = t_in.at[k, pl.ds(7 * OFF[c] + s * 2 * p, 2 * p)]
                branch_in[k, c].append(send(place, target, ts_send, ts_recv, (k, c, s), device))
        else:
            for s, device in enumerate(t_to):
                place = t_out.at[k, rows_at(8 * OFF[c] + device[1] * p, p)]
                target = t_in.at[k, pl.ds(7 * OFF[c] + s * p, p)]
                branch_in[k, c].append(send(place, target, ts_send, ts_recv, (k, c, s), device))

    def halve_tokens(k, c):
        p = OWN[c]
        for copy in branch_in[k, c]:
            copy.wait_recv()

        def total(sub):
            value = t_out[k, rows_at(8 * OFF[c] + (yi * 2 + sub) * p, p), :].astype(F32)
            for s in range(3):
                value = value + t_in[k, rows_at(7 * OFF[c] + s * 2 * p + sub * p, p), :].astype(F32)
            return value

        place = rows_at(8 * OFF[c] + (yi * 2 + 1 - zl) * p, p)
        t_out[k, place, :] = total(1 - zl).astype(BF16)
        half_in[k, c] = send(
            t_out.at[k, place], t_in.at[k, pl.ds(7 * OFF[c] + 6 * p, p)], tr_send, tr_recv, (k, c), t_pair
        )
        t_acc[k, OFF[c] : OFF[c] + p, :] = total(zl)

    def finish_tokens(k, c):
        p = OWN[c]
        rows = slice(OFF[c], OFF[c] + p)
        if c in R_PAIRS:
            half_in[k, c].wait_recv()
            value = t_acc[k, rows, :] + t_in[k, 7 * OFF[c] + 6 * p : 7 * OFF[c] + 7 * p, :].astype(F32)
        else:
            for copy in branch_in[k, c]:
                copy.wait_recv()
            value = t_out[k, rows_at(8 * OFF[c] + tensor * p, p), :].astype(F32)
            for s in range(7):
                value = value + t_in[k, 7 * OFF[c] + s * p : 7 * OFF[c] + (s + 1) * p, :].astype(F32)
        if k:
            grad_normed[rows, :] = value
        else:
            branch_ref[rows, :] = (value + b_down_ref[...].reshape(1, WIDE)).astype(BF16)

    stores = {}

    def store(k, slot, source, target):
        copy = pltpu.make_async_copy(source, target, store_sem.at[k, slot])
        copy.start()
        stores[k, slot] = copy

    def weight_up(_, j):
        slot = j % 2
        if (1, slot) in stores:
            stores[1, slot].wait()
        strip = full[1, j // 3, :, (j % 3) * STRIP : (j % 3 + 1) * STRIP]
        gu_tile[slot] = dot_transposed(nrm[...], strip).astype(BF16)
        store(1, slot, gu_tile.at[slot], gw_up_hbm.at[:, pl.ds(j * STRIP, STRIP)])
        ones = jnp.ones((8, TOKENS), BF16)
        grad_b_up_ref[j * STRIP : (j + 1) * STRIP] = jnp.dot(ones, strip, preferred_element_type=F32)[0]
        if j == 0:
            grad_b_down_ref[...] = jnp.dot(ones, dbr[...], preferred_element_type=F32)[0]

    def weight_down(_, j):
        slot = j % 2
        if (0, slot) in stores:
            stores[0, slot].wait()
        strip = full[0, j // 3, :, (j % 3) * STRIP : (j % 3 + 1) * STRIP]
        gd_tile[slot] = dot_transposed(strip, dbr[...]).astype(BF16)
        store(0, slot, gd_tile.at[slot], gw_down_hbm.at[pl.ds(j * STRIP, STRIP)])

    def back_sums(k, c):
        gn, std = grad_normed[...], standard[...]
        scaled = gn * gain_ref[...].reshape(1, WIDE)
        back_stats[0] = columns_to_rows(
            jnp.sum(scaled, axis=1, keepdims=True), jnp.sum(scaled * std, axis=1, keepdims=True)
        )
        small["back"] = [
            send(back_stats.at[0], back_stats.at[s + 1], bs_send, bs_recv, s, device) for s, device in enumerate(d_to)
        ]
        gb[0, 0:1, :] = jnp.sum(gn * std, axis=0, keepdims=True)
        gb[0, 1:2, :] = jnp.sum(gn, axis=0, keepdims=True)
        gb[0, 2:8, :] = jnp.zeros((6, WIDE), F32)
        small["gains"] = [send(gb.at[0], gb.at[s + 1], gb_send, gb_recv, s, device) for s, device in enumerate(t_to)]

    def grad_inputs(k, c):
        for copy in small["back"]:
            copy.wait_recv()
        first = functools.reduce(jnp.add, [back_stats[s, 0:1, :] for s in range(16)]) / D
        second = functools.reduce(jnp.add, [back_stats[s, 1:2, :] for s in range(16)]) / D
        first, second = rows_to_columns(first, second)
        scaled = grad_normed[...] * gain_ref[...].reshape(1, WIDE)
        grad_in_ref[...] = (inverse_ref[:, 0:1] * (scaled - first - standard[...] * second)).astype(BF16)
        for copy in small["gains"]:
            copy.wait_recv()
        both = functools.reduce(jnp.add, [gb[s] for s in range(8)])
        grad_gain_ref[...] = both[0]
        grad_bias_ref[...] = both[1]

    steps = {
        "TZ": pair_tokens, "TY": gather_tokens, "ST": statistics, "NM": normalise, "M": multiply, "A": add_core,
        "B": add_first, "C": add_second, "G": activate, "E1": gather_first, "E2": gather_second, "E3": gather_third,
        "F": multiply_back, "H1": halve_tokens, "H": finish_tokens, "WU": weight_up, "WD": weight_down,
        "S": back_sums, "Z": grad_inputs,
    }
    for name, k, c in ORDER:
        steps[name](k, c)
    for copy in stores.values():
        copy.wait()
    for copy in sent:
        copy.wait_send()


def on_device(inputs, norm_gain, norm_bias, w_up, b_up, w_down, b_down, d_branch):
    vmem = pl.BlockSpec(memory_space=pltpu.VMEM)
    hbm = pl.BlockSpec(memory_space=pl.ANY)
    shape = jax.ShapeDtypeStruct

    def pair(*size):
        return [pltpu.SemaphoreType.DMA(size)] * 2

    branch, grad_in, grad_gain, grad_bias, grad_b_up, grad_b_down, grad_w_up, grad_w_down = pl.pallas_call(
        kernel,
        out_shape=(
            shape((128, WIDE), BF16), shape((128, WIDE), BF16), shape((WIDE,), F32), shape((WIDE,), F32),
            shape((2 * HALF,), F32), shape((WIDE,), F32), shape((WIDE, 2 * HALF), BF16), shape((2 * HALF, WIDE), BF16),
        ),
        in_specs=[vmem] * 6 + [hbm] * 2,
        out_specs=(vmem,) * 6 + (hbm,) * 2,
        scratch_shapes=[
            pltpu.VMEM((2, WIDE, HALF), BF16),
            pltpu.VMEM((2, HALF, WIDE), BF16),
            pltpu.VMEM((TOKENS, WIDE), BF16),
            pltpu.VMEM((TOKENS, WIDE), BF16),
            pltpu.VMEM((2, 2, TOKENS, HALF), BF16),
            pltpu.VMEM((2, TOKENS, HALF), BF16),
            pltpu.VMEM((2, 2, 128, HALF), BF16),
            pltpu.VMEM((2, 2, 256, HALF), BF16),
            pltpu.VMEM((2, sum(Z_ROWS), HALF), BF16),
            pltpu.VMEM((2, 2, TOKENS, HALF), BF16),
            pltpu.VMEM((2, TOKENS, WIDE), BF16),
            pltpu.VMEM((2, 7 * 128, WIDE), BF16),
            pltpu.VMEM((2, 128, WIDE), F32),
            pltpu.VMEM((128, WIDE), F32),
            pltpu.VMEM((128, WIDE), F32),
            pltpu.VMEM((128, 128), F32),
            pltpu.VMEM((16, 8, 128), F32),
            pltpu.VMEM((16, 8, 128), F32),
            pltpu.VMEM((8, 8, WIDE), F32),
            pltpu.VMEM((2, WIDE, STRIP), BF16),
            pltpu.VMEM((2, STRIP, WIDE), BF16),
            pltpu.SemaphoreType.DMA((3,)), pltpu.SemaphoreType.DMA((2, 2)),
            *pair(2, CHUNKS, 7),
            *pair(2, CHUNKS),
            *pair(2, CHUNKS),
            *pair(2, CHUNKS, 2),
            *pair(2, CHUNKS, 2),
            *pair(2, CHUNKS),
            *pair(2, CHUNKS, 2),
            *pair(2, CHUNKS, 2),
            *pair(2, CHUNKS, 2),
            *pair(2, CHUNKS, 4),
            *pair(2, CHUNKS, 7),
            *pair(2, CHUNKS),
            *pair(15), *pair(15), *pair(7),
        ],
        compiler_params=pltpu.CompilerParams(collective_id=0, has_side_effects=True, vmem_limit_bytes=63 * 2**20),
    )(inputs, norm_gain, norm_bias, b_up, b_down, d_branch, w_up, w_down.reshape(2, HALF, WIDE))
    return branch, grad_in, grad_w_up, grad_b_up, grad_w_down, grad_b_down, grad_gain, grad_bias


def solution(mesh):
    placed = (
        P("tensor", "dp"), P("dp"), P("dp"), P("dp", "tensor"), P("tensor"), P("tensor", "dp"), P("dp"), P("tensor", "dp"),
    )
    return jax.shard_map(
        on_device,
        mesh=mesh,
        in_specs=placed,
        out_specs=(
            P("tensor", "dp"), P("tensor", "dp"), P("dp", "tensor"), P("tensor"), P("tensor", "dp"), P("dp"), P("dp"), P("dp"),
        ),
        check_vma=False,
    )
```

```python
import functools

import jax
import jax.numpy as jnp
from jax import lax
from jax.experimental import pallas as pl
from jax.experimental.pallas import tpu as pltpu
from jax.sharding import PartitionSpec as P

MESH = pl.DeviceIdType.MESH
F32, BF16 = jnp.float32, jnp.bfloat16

D = 12288
WIDE = 768
HALF = 1536
TOKENS = 1024
STRIP = 512
K0 = 0.7978845608028654
K1 = 0.044715

OWN = (16, 32, 32, 32, 16)
CHUNKS = len(OWN)
OFF = tuple(sum(OWN[:c]) for c in range(CHUNKS))
Z_FIRST = (2,)
T_PAIRS = (1, 2, 3, 4)
R_PAIRS = (0, 1, 2)
Z_ROWS = tuple((4 if c in Z_FIRST else 1) * OWN[c] for c in range(CHUNKS))
Z_OFF = tuple(sum(Z_ROWS[:c]) for c in range(CHUNKS))

ORDER = (
    ("TZ", 0, 1), ("TZ", 0, 3), ("TY", 0, 0), ("ST", 0, 0), ("TY", 0, 1), ("TY", 0, 3), ("NM", 0, 0), ("TZ", 0, 2),
    ("TZ", 0, 4), ("M", 0, 0), ("TY", 1, 0), ("TZ", 1, 1), ("A", 0, 0), ("M", 0, 1), ("TZ", 1, 2), ("TZ", 1, 3),
    ("TY", 0, 2), ("B", 0, 0), ("TY", 0, 4), ("A", 0, 1), ("M", 0, 3), ("M", 1, 0), ("A", 0, 3), ("C", 0, 0),
    ("A", 1, 0), ("TY", 1, 1), ("TY", 1, 2), ("B", 0, 1), ("M", 0, 2), ("M", 0, 4), ("B", 0, 3), ("TZ", 1, 4),
    ("A", 0, 2), ("A", 0, 4), ("TY", 1, 4), ("B", 1, 0), ("M", 1, 1), ("TY", 1, 3), ("A", 1, 1), ("M", 1, 2),
    ("C", 0, 1), ("B", 0, 4), ("M", 1, 4), ("C", 1, 0), ("B", 0, 2), ("B", 1, 1), ("A", 1, 2), ("M", 1, 3),
    ("A", 1, 3), ("A", 1, 4), ("G", 0, 0), ("C", 0, 2), ("C", 1, 1), ("B", 1, 3), ("E1", 0, 0), ("B", 1, 4),
    ("B", 1, 2), ("G", 0, 1), ("E2", 0, 0), ("C", 0, 3), ("E1", 1, 0), ("C", 1, 3), ("C", 1, 2), ("E1", 0, 1),
    ("E1", 1, 1), ("E3", 0, 0), ("G", 0, 3), ("G", 0, 2), ("C", 0, 4), ("E2", 0, 1), ("C", 1, 4), ("E1", 1, 2),
    ("E2", 1, 1), ("G", 0, 4), ("E2", 1, 0), ("E3", 0, 1), ("E1", 0, 2), ("E2", 1, 2), ("E1", 1, 3), ("F", 0, 0),
    ("F", 0, 1), ("E1", 1, 4), ("E3", 1, 1), ("E2", 0, 2), ("E3", 1, 0), ("F", 1, 1), ("E1", 0, 4), ("F", 1, 0),
    ("E2", 1, 3), ("E1", 0, 3), ("E3", 1, 2), ("H1", 0, 0), ("H1", 0, 1), ("F", 1, 2), ("E3", 1, 3), ("H1", 1, 1),
    ("E2", 1, 4), ("E2", 0, 4), ("F", 1, 3), ("E2", 0, 3), ("H1", 1, 0), ("E3", 1, 4), ("H", 0, 0), ("E3", 0, 2),
    ("E3", 0, 4), ("F", 1, 4), ("F", 0, 4), ("E3", 0, 3), ("F", 0, 2), ("H1", 1, 2), ("H", 1, 1), ("H", 1, 3),
    ("F", 0, 3), ("H", 1, 4), ("WD", 0, 1), ("H", 1, 2), ("H", 1, 0), ("S", 0, 0), ("H", 0, 4), ("H1", 0, 2),
    ("WD", 0, 0), ("Z", 0, 0), ("H", 0, 2), ("H", 0, 1), ("H", 0, 3),
)


def transposed_dot(left, right):
    return lax.dot_general(left, right, (((1,), (1,)), ((), ())), preferred_element_type=F32)


def dot_transposed(left, right):
    return lax.dot_general(left, right, (((0,), (0,)), ((), ())), preferred_element_type=F32)


def columns_to_rows(first, second):
    lane = lax.broadcasted_iota(jnp.int32, (128, 128), 1)
    return jnp.where(lane == 0, first, jnp.where(lane == 1, second, 0.0)).T[0:8, :]


def rows_to_columns(first, second):
    row = lax.broadcasted_iota(jnp.int32, (128, 128), 0)
    both = jnp.where(row == 0, first, jnp.where(row == 1, second, 0.0)).T
    return both[:, 0:1], both[:, 1:2]


def column_sums(load, width):
    def block(i, total):
        return total + load(pl.ds(pl.multiple_of(i * 16, 16), 16)).astype(F32)

    return jnp.sum(lax.fori_loop(0, TOKENS // 16, block, jnp.zeros((16, width), F32)), axis=0)


def kernel(
    x_ref, gain_ref, bias_ref, b_up_ref, b_down_ref, d_ref, w_up_hbm, w_down_hbm,
    branch_ref, grad_in_ref, grad_gain_ref, grad_bias_ref, grad_b_down_ref, gw_down_hbm, gh_hbm, nrm_hbm,
    w_up, w_down, dbr, nrm, part, core_in, x1_in, x2_in, z_in, full, t_out, t_in, t_acc,
    standard, grad_normed, inverse_ref, stats, back_stats, gb,
    load_sem, store_sem, t_send, t_recv, tz_send, tz_recv, core_send, core_recv, x1_send, x1_recv, x2_send, x2_recv,
    z_send, z_recv, ga_send, ga_recv, gx_send, gx_recv, gf_send, gf_recv, gc_send, gc_recv,
    ts_send, ts_recv, tr_send, tr_recv, st_send, st_recv, bs_send, bs_recv, gb_send, gb_recv,
):
    dp, tensor = lax.axis_index("dp"), lax.axis_index("tensor")
    xi, zh, core = dp // 4, (dp // 2) % 2, dp % 2
    yi, zl = tensor // 2, tensor % 2
    x_right, x_left, x_far = (xi + 1) % 4, (xi + 3) % 4, (xi + 2) % 4
    right = (x_right * 4 + zh * 2 + core, tensor)
    left = (x_left * 4 + zh * 2 + core, tensor)
    across = (xi * 4 + (1 - zh) * 2 + core, tensor)
    sibling = (xi * 4 + zh * 2 + (1 - core), tensor)
    t_pair = (dp, yi * 2 + (1 - zl))
    y_to = [(dp, ((yi + dy) % 4) * 2 + zl) for dy in (1, 2, 3)]
    t_to = y_to + [t_pair] + [(dp, ((yi + dy) % 4) * 2 + (1 - zl)) for dy in (1, 2, 3)]
    d_to = []
    for dx in range(4):
        for mz in range(2):
            for mc in range(2):
                if dx or mz or mc:
                    d_to.append((((xi + dx) % 4) * 4 + (1 - zh if mz else zh) * 2 + (1 - core if mc else core), tensor))

    loads = [[pltpu.make_async_copy(w_down_hbm, w_down, load_sem.at[0])]]
    loads.append([pltpu.make_async_copy(w_up_hbm.at[:, pl.ds(h * HALF, HALF)], w_up.at[h], load_sem.at[1 + h]) for h in range(2)])
    for copy in loads[0] + loads[1]:
        copy.start()

    barrier = pltpu.get_barrier_semaphore()
    for device in t_to + d_to:
        pl.semaphore_signal(barrier, inc=1, device_id=device, device_id_type=MESH)

    def rows_at(at, count):
        return pl.ds(pl.multiple_of(at, 16), count)

    for c in range(CHUNKS):
        dbr[rows_at(8 * OFF[c] + tensor * OWN[c], OWN[c]), :] = d_ref[OFF[c] : OFF[c] + OWN[c], :]
    pl.semaphore_wait(barrier, len(t_to) + len(d_to))

    sent = []

    def send(source, target, sends, receives, index, device):
        copy = pltpu.make_async_remote_copy(
            src_ref=source, dst_ref=target, send_sem=sends.at[index], recv_sem=receives.at[index],
            device_id=device, device_id_type=MESH,
        )
        copy.start()
        sent.append(copy)
        return copy

    stores = []

    def store(source, target):
        copy = pltpu.make_async_copy(source, target, store_sem.at[len(stores)])
        copy.start()
        stores.append(copy)

    pair_in, token_in, core_arrives, x1_arrives, x2_arrives, z_arrives = {}, {}, {}, {}, {}, {}
    own_in, neighbour_in, far_in, core_full, branch_in, half_in = {}, {}, {}, {}, {}, {}
    small = {}
    tokens = (dbr, nrm)

    def pair_tokens(k, c):
        place = tokens[k].at[rows_at(8 * OFF[c] + tensor * OWN[c], OWN[c])]
        pair_in[k, c] = send(place, place, tz_send, tz_recv, (k, c), t_pair)

    def gather_tokens(k, c):
        if c in T_PAIRS:
            pair_in[k, c].wait_recv()
            place = tokens[k].at[rows_at(8 * OFF[c] + yi * 2 * OWN[c], 2 * OWN[c])]
            to = y_to
        else:
            place = tokens[k].at[rows_at(8 * OFF[c] + tensor * OWN[c], OWN[c])]
            to = t_to
        token_in[k, c] = [send(place, place, t_send, t_recv, (k, c, s), device) for s, device in enumerate(to)]

    def statistics(k, c):
        widened = x_ref[...].astype(F32)
        total = jnp.sum(widened, axis=1, keepdims=True)
        off = widened - total / WIDE
        stats[0] = columns_to_rows(total, jnp.sum(off * off, axis=1, keepdims=True))
        small["forward"] = [send(stats.at[0], stats.at[s + 1], st_send, st_recv, s, device) for s, device in enumerate(d_to)]

    def normalise(k, c):
        for copy in small["forward"]:
            copy.wait_recv()
        sums = [stats[s, 0:1, :] for s in range(16)]
        mean = functools.reduce(jnp.add, sums) / D
        spread = jnp.zeros_like(mean)
        for s in range(16):
            apart = sums[s] / WIDE - mean
            spread = spread + (stats[s, 1:2, :] + WIDE * (apart * apart))
        mean, inverse = rows_to_columns(mean, lax.rsqrt(spread / D + 1e-05))
        inverse_ref[...] = jnp.broadcast_to(inverse, (128, 128))
        gain, bias = gain_ref[...].reshape(1, WIDE), bias_ref[...].reshape(1, WIDE)
        for c in range(CHUNKS):
            rows = slice(OFF[c], OFF[c] + OWN[c])
            std = (x_ref[rows, :].astype(F32) - mean[rows]) * inverse[rows]
            standard[rows, :] = std
            nrm[rows_at(8 * OFF[c] + tensor * OWN[c], OWN[c]), :] = (std * gain + bias).astype(BF16)

    def accumulate(k, c, start, count, others):
        size = 32 if count % 32 == 0 else 16

        def block(i, _):
            at = i * size
            rows = rows_at(8 * OFF[c] + start + at, size)
            value = part[k, core, rows, :].astype(F32)
            for load in others:
                value = value + load(at, size).astype(F32)
            part[k, core, rows, :] = value.astype(BF16)
            return 0

        if count == size:
            block(0, 0)
        else:
            lax.fori_loop(0, count // size, block, 0)

    def multiply(k, c):
        if (k, c) == (k, 0):
            for copy in loads[k]:
                copy.wait()
        for copy in token_in[k, c]:
            copy.wait_recv()
        rows = pl.ds(8 * OFF[c], 8 * OWN[c])
        core_arrives[k, c] = pltpu.make_async_remote_copy(
            src_ref=part.at[k, 1 - core, rows], dst_ref=core_in.at[k, rows], send_sem=core_send.at[k, c],
            recv_sem=core_recv.at[k, c], device_id=sibling, device_id_type=MESH,
        )
        sent.append(core_arrives[k, c])

        def one(step, _):
            half = (1 - core) * (1 - step) + core * step
            if k:
                value = jnp.dot(nrm[rows, :], w_up[half], preferred_element_type=F32)
            else:
                value = transposed_dot(dbr[rows, :], w_down[half])
            part[k, half, rows, :] = value.astype(BF16)

            @pl.when(step == 0)
            def _():
                core_arrives[k, c].start()

            return 0

        lax.fori_loop(0, 2, one, 0)

    def part_rows(k, c, start, count):
        return part.at[k, core, rows_at(8 * OFF[c] + start, count)]

    def add_core(k, c):
        p = OWN[c]
        core_arrives[k, c].wait_recv()

        def add(start, count):
            accumulate(k, c, start, count, [lambda at, size: core_in[k, rows_at(8 * OFF[c] + start + at, size), :]])

        if c in Z_FIRST:
            add((1 - zh) * 4 * p, 4 * p)
            z_arrives[k, c] = send(
                part_rows(k, c, (1 - zh) * 4 * p, 4 * p), z_in.at[k, pl.ds(Z_OFF[c], 4 * p)], z_send, z_recv, (k, c), across
            )
            add(zh * 4 * p, 4 * p)
        else:
            add(x_far * 2 * p, 2 * p)
            x1_arrives[k, c] = [
                send(
                    part_rows(k, c, x_far * 2 * p + side * p, p), x1_in.at[k, side, pl.ds(OFF[c], p)],
                    x1_send, x1_recv, (k, c, side), device,
                )
                for side, device in enumerate((right, left))
            ]
            for piece in (x_right, x_left, xi):
                add(piece * 2 * p, 2 * p)

    def add_first(k, c):
        p = OWN[c]
        if c in Z_FIRST:
            z_arrives[k, c].wait_recv()

            def add(piece):
                start = piece * p
                accumulate(
                    k, c, zh * 4 * p + start, p, [lambda at, size: z_in[k, rows_at(Z_OFF[c] + start + at, size), :]]
                )

            add(x_far)
            x1_arrives[k, c] = [
                send(
                    part_rows(k, c, zh * 4 * p + x_far * p + side * (p // 2), p // 2),
                    x1_in.at[k, side, pl.ds(OFF[c], p // 2)], x1_send, x1_recv, (k, c, side), device,
                )
                for side, device in enumerate((right, left))
            ]
            for piece in (x_right, x_left, xi):
                add(piece)
        else:
            add_x1(k, c, 2 * p, 0)

    def add_x1(k, c, size, base):
        x2_arrives[k, c] = []
        for side, (piece, device) in enumerate(((x_right, right), (x_left, left))):
            x1_arrives[k, c][side].wait_recv()
            accumulate(
                k, c, base + piece * size + side * (size // 2), size // 2,
                [lambda at, count, side=side: x1_in[k, side, rows_at(OFF[c] + at, count), :]],
            )
            x2_arrives[k, c].append(
                send(
                    part_rows(k, c, base + piece * size, size), x2_in.at[k, side, pl.ds(2 * OFF[c], size)],
                    x2_send, x2_recv, (k, c, side), device,
                )
            )

    def add_second(k, c):
        p = OWN[c]
        if c in Z_FIRST:
            add_x1(k, c, p, zh * 4 * p)
            return
        for copy in x2_arrives[k, c]:
            copy.wait_recv()

        def add(sub):
            start = sub * p
            accumulate(
                k, c, xi * 2 * p + start, p,
                [lambda at, size, side=side: x2_in[k, side, rows_at(2 * OFF[c] + start + at, size), :] for side in range(2)],
            )

        add(1 - zh)
        z_arrives[k, c] = send(
            part_rows(k, c, xi * 2 * p + (1 - zh) * p, p), z_in.at[k, pl.ds(Z_OFF[c], p)], z_send, z_recv, (k, c), across
        )
        add(zh)

    def activate(_, c):
        p = OWN[c]
        if c in Z_FIRST:
            mine = zh * 4 * p + xi * p
            for k in range(2):
                for copy in x2_arrives[k, c]:
                    copy.wait_recv()
        else:
            mine = xi * 2 * p + zh * p
            for k in range(2):
                z_arrives[k, c].wait_recv()
        bias = b_up_ref[pl.ds(pl.multiple_of(core * HALF, HALF), HALF)].reshape(1, HALF)

        def total(k, at):
            value = part[k, core, rows_at(8 * OFF[c] + mine + at, 16), :].astype(F32)
            if c in Z_FIRST:
                for side in range(2):
                    value = value + x2_in[k, side, rows_at(2 * OFF[c] + at, 16), :].astype(F32)
                return value
            return value + z_in[k, rows_at(Z_OFF[c] + at, 16), :].astype(F32)

        def block(i, _):
            at = i * 16
            rows = rows_at(8 * OFF[c] + mine + at, 16)
            h = total(1, at) + bias
            square = h * h
            t = jnp.tanh(K0 * (h + K1 * (square * h)))
            full[0, core, rows, :] = (0.5 * h * (1.0 + t)).astype(BF16)
            slope = 0.5 * (1.0 + t) + 0.5 * h * (1.0 - t * t) * (K0 * (1.0 + 3.0 * K1 * square))
            full[1, core, rows, :] = (total(0, at) * slope).astype(BF16)
            return 0

        lax.fori_loop(0, p // 16, block, 0)
        for k in (1, 0):
            place = full.at[k, core, rows_at(8 * OFF[c] + mine, p)]
            to = (right, left) if c in Z_FIRST else (across,)
            own_in[k, c] = [send(place, place, ga_send, ga_recv, (k, c, s), device) for s, device in enumerate(to)]

    def full_rows(k, c, start, count):
        return full.at[k, core, rows_at(8 * OFF[c] + start, count)]

    def to_sibling(k, c, start, count):
        arrivals = core_full.setdefault((k, c), [])
        place = full_rows(k, c, start, count)
        arrivals.append(send(place, place, gc_send, gc_recv, (k, c, len(arrivals)), sibling))

    def forward(k, c, arrivals, size, base):
        made = []
        for side, (piece, device) in enumerate(((x_left, right), (x_right, left))):
            arrivals[side].wait_recv()
            place = full_rows(k, c, base + piece * size + side * (size // 2), size // 2)
            made.append(send(place, place, gf_send, gf_recv, (k, c, side), device))
        return made

    def gather_first(k, c):
        p = OWN[c]
        if c in Z_FIRST:
            far_in[k, c] = forward(k, c, own_in[k, c], p, zh * 4 * p)
        else:
            own_in[k, c][0].wait_recv()
            place = full_rows(k, c, xi * 2 * p, 2 * p)
            neighbour_in[k, c] = [
                send(place, place, gx_send, gx_recv, (k, c, side), device) for side, device in enumerate((right, left))
            ]
            to_sibling(k, c, xi * 2 * p, 2 * p)

    def gather_second(k, c):
        p = OWN[c]
        if c in Z_FIRST:
            for copy in far_in[k, c]:
                copy.wait_recv()
            place = full_rows(k, c, zh * 4 * p, 4 * p)
            neighbour_in[k, c] = [send(place, place, gx_send, gx_recv, (k, c, 0), across)]
            to_sibling(k, c, zh * 4 * p, 4 * p)
        else:
            far_in[k, c] = forward(k, c, neighbour_in[k, c], 2 * p, 0)
            for piece in (x_left, x_right):
                to_sibling(k, c, piece * 2 * p, 2 * p)

    def gather_third(k, c):
        p = OWN[c]
        if c in Z_FIRST:
            neighbour_in[k, c][0].wait_recv()
            to_sibling(k, c, (1 - zh) * 4 * p, 4 * p)
        else:
            for copy in far_in[k, c]:
                copy.wait_recv()
            to_sibling(k, c, x_far * 2 * p, 2 * p)

    def multiply_back(k, c):
        p = OWN[c]
        for copy in core_full[k, c]:
            copy.wait_recv()
        rows = pl.ds(8 * OFF[c], 8 * p)

        def tile(j, _):
            at = pl.ds(pl.multiple_of(j * 256, 256), 256)
            if k:
                value = transposed_dot(full[1, 0, rows, :], w_up[0, at, :])
                value += transposed_dot(full[1, 1, rows, :], w_up[1, at, :])
            else:
                value = jnp.dot(full[0, 0, rows, :], w_down[0, :, at], preferred_element_type=F32)
                value += jnp.dot(full[0, 1, rows, :], w_down[1, :, at], preferred_element_type=F32)
            t_out[k, rows, at] = value.astype(BF16)
            return 0

        lax.fori_loop(0, WIDE // 256, tile, 0)
        if k:
            for half in range(2):
                store(full.at[1, half, rows], gh_hbm.at[rows, pl.ds(half * HALF, HALF)])
            store(nrm.at[rows], nrm_hbm.at[rows])
        branch_in[k, c] = []
        if c in R_PAIRS:
            for s, device in enumerate(y_to):
                place = t_out.at[k, rows_at(8 * OFF[c] + (device[1] // 2) * 2 * p, 2 * p)]
                target = t_in.at[k, pl.ds(7 * OFF[c] + s * 2 * p, 2 * p)]
                branch_in[k, c].append(send(place, target, ts_send, ts_recv, (k, c, s), device))
        else:
            for s, device in enumerate(t_to):
                place = t_out.at[k, rows_at(8 * OFF[c] + device[1] * p, p)]
                target = t_in.at[k, pl.ds(7 * OFF[c] + s * p, p)]
                branch_in[k, c].append(send(place, target, ts_send, ts_recv, (k, c, s), device))

    def halve_tokens(k, c):
        p = OWN[c]
        for copy in branch_in[k, c]:
            copy.wait_recv()

        def total(sub):
            value = t_out[k, rows_at(8 * OFF[c] + (yi * 2 + sub) * p, p), :].astype(F32)
            for s in range(3):
                value = value + t_in[k, rows_at(7 * OFF[c] + s * 2 * p + sub * p, p), :].astype(F32)
            return value

        place = rows_at(8 * OFF[c] + (yi * 2 + 1 - zl) * p, p)
        t_out[k, place, :] = total(1 - zl).astype(BF16)
        half_in[k, c] = send(
            t_out.at[k, place], t_in.at[k, pl.ds(7 * OFF[c] + 6 * p, p)], tr_send, tr_recv, (k, c), t_pair
        )
        t_acc[k, OFF[c] : OFF[c] + p, :] = total(zl)

    def finish_tokens(k, c):
        p = OWN[c]
        rows = slice(OFF[c], OFF[c] + p)
        if c in R_PAIRS:
            half_in[k, c].wait_recv()
            value = t_acc[k, rows, :] + t_in[k, 7 * OFF[c] + 6 * p : 7 * OFF[c] + 7 * p, :].astype(F32)
        else:
            for copy in branch_in[k, c]:
                copy.wait_recv()
            value = t_out[k, rows_at(8 * OFF[c] + tensor * p, p), :].astype(F32)
            for s in range(7):
                value = value + t_in[k, 7 * OFF[c] + s * p : 7 * OFF[c] + (s + 1) * p, :].astype(F32)
        if k:
            grad_normed[rows, :] = value
        else:
            branch_ref[rows, :] = (value + b_down_ref[...].reshape(1, WIDE)).astype(BF16)

    def weight_down(_, half):
        def strip(i, _):
            at = pl.ds(pl.multiple_of(i * STRIP, STRIP), STRIP)
            w_down[half, at, :] = dot_transposed(full[0, half, :, at], dbr[...]).astype(BF16)
            return 0

        lax.fori_loop(0, HALF // STRIP, strip, 0)
        store(w_down.at[half], gw_down_hbm.at[pl.ds(half * HALF, HALF)])
        if half == 0:
            grad_b_down_ref[...] = column_sums(lambda rows: dbr[rows, :], WIDE)

    def back_sums(k, c):
        gn, std = grad_normed[...], standard[...]
        scaled = gn * gain_ref[...].reshape(1, WIDE)
        back_stats[0] = columns_to_rows(
            jnp.sum(scaled, axis=1, keepdims=True), jnp.sum(scaled * std, axis=1, keepdims=True)
        )
        small["back"] = [
            send(back_stats.at[0], back_stats.at[s + 1], bs_send, bs_recv, s, device) for s, device in enumerate(d_to)
        ]
        gb[0, 0:1, :] = jnp.sum(gn * std, axis=0, keepdims=True)
        gb[0, 1:2, :] = jnp.sum(gn, axis=0, keepdims=True)
        gb[0, 2:8, :] = jnp.zeros((6, WIDE), F32)
        small["gains"] = [send(gb.at[0], gb.at[s + 1], gb_send, gb_recv, s, device) for s, device in enumerate(t_to)]

    def grad_inputs(k, c):
        for copy in small["back"]:
            copy.wait_recv()
        first = functools.reduce(jnp.add, [back_stats[s, 0:1, :] for s in range(16)]) / D
        second = functools.reduce(jnp.add, [back_stats[s, 1:2, :] for s in range(16)]) / D
        first, second = rows_to_columns(first, second)
        scaled = grad_normed[...] * gain_ref[...].reshape(1, WIDE)
        grad_in_ref[...] = (inverse_ref[:, 0:1] * (scaled - first - standard[...] * second)).astype(BF16)
        for copy in small["gains"]:
            copy.wait_recv()
        both = functools.reduce(jnp.add, [gb[s] for s in range(8)])
        grad_gain_ref[...] = both[0]
        grad_bias_ref[...] = both[1]

    steps = {
        "TZ": pair_tokens, "TY": gather_tokens, "ST": statistics, "NM": normalise, "M": multiply, "A": add_core,
        "B": add_first, "C": add_second, "G": activate, "E1": gather_first, "E2": gather_second, "E3": gather_third,
        "F": multiply_back, "H1": halve_tokens, "H": finish_tokens, "WD": weight_down,
        "S": back_sums, "Z": grad_inputs,
    }
    for name, k, c in ORDER:
        steps[name](k, c)
    for copy in stores:
        copy.wait()
    for copy in sent:
        copy.wait_send()


def last_kernel(
    nrm_hbm, gh_hbm, gw_down_hbm, branch_in, grad_in_in, gain_in, bias_in, b_down_in,
    branch_out, grad_in_out, gw_up_out, b_up_out, gw_down_out, b_down_out, gain_out, bias_out,
    nrm, gh, gw_up, gw_down, branch, grad_in, gain, bias, b_down, in_sem, out_sem,
):
    strips, parts = 2 * HALF // STRIP, 4

    def columns(i):
        return pl.ds(i * STRIP, STRIP)

    ins, outs = [], []

    def fetch(source, target):
        copy = pltpu.make_async_copy(source, target, in_sem.at[len(ins)])
        copy.start()
        ins.append(copy)
        return copy

    def put(source, target):
        copy = pltpu.make_async_copy(source, target, out_sem.at[len(outs)])
        copy.start()
        outs.append(copy)

    first = fetch(nrm_hbm, nrm)
    strip_in = [fetch(gh_hbm.at[:, columns(i)], gh.at[i]) for i in range(strips)]
    rows = [pl.ds(i * (2 * HALF // parts), 2 * HALF // parts) for i in range(parts)]
    passing = [(fetch(gw_down_hbm.at[r], gw_down.at[r]), gw_down.at[r], gw_down_out.at[r]) for r in rows]
    for source, held, target in (
        (branch_in, branch, branch_out), (grad_in_in, grad_in, grad_in_out), (gain_in, gain, gain_out),
        (bias_in, bias, bias_out), (b_down_in, b_down, b_down_out),
    ):
        passing.append((fetch(source, held), held, target))
    first.wait()
    for i in range(strips):
        strip_in[i].wait()
        b_up_out[i * STRIP : (i + 1) * STRIP] = column_sums(lambda r: gh[i, r, :], STRIP)
        gw_up[i] = dot_transposed(nrm[...], gh[i]).astype(BF16)
        put(gw_up.at[i], gw_up_out.at[:, columns(i)])
        if i >= 2:
            for copy, held, target in passing[(i - 2) * 3 : (i - 1) * 3]:
                copy.wait()
                put(held, target)
    for copy in outs:
        copy.wait()


def on_device(inputs, norm_gain, norm_bias, w_up, b_up, w_down, b_down, d_branch):
    vmem = pl.BlockSpec(memory_space=pltpu.VMEM)
    hbm = pl.BlockSpec(memory_space=pl.ANY)
    shape = jax.ShapeDtypeStruct

    def pair(*size):
        return [pltpu.SemaphoreType.DMA(size)] * 2

    branch, grad_in, grad_gain, grad_bias, grad_b_down, grad_w_down, gh, nrm = pl.pallas_call(
        kernel,
        out_shape=(
            shape((128, WIDE), BF16), shape((128, WIDE), BF16), shape((WIDE,), F32), shape((WIDE,), F32),
            shape((WIDE,), F32), shape((2 * HALF, WIDE), BF16), shape((TOKENS, 2 * HALF), BF16), shape((TOKENS, WIDE), BF16),
        ),
        in_specs=[vmem] * 6 + [hbm] * 2,
        out_specs=(vmem,) * 5 + (hbm,) * 3,
        scratch_shapes=[
            pltpu.VMEM((2, WIDE, HALF), BF16),
            pltpu.VMEM((2, HALF, WIDE), BF16),
            pltpu.VMEM((TOKENS, WIDE), BF16),
            pltpu.VMEM((TOKENS, WIDE), BF16),
            pltpu.VMEM((2, 2, TOKENS, HALF), BF16),
            pltpu.VMEM((2, TOKENS, HALF), BF16),
            pltpu.VMEM((2, 2, 128, HALF), BF16),
            pltpu.VMEM((2, 2, 256, HALF), BF16),
            pltpu.VMEM((2, sum(Z_ROWS), HALF), BF16),
            pltpu.VMEM((2, 2, TOKENS, HALF), BF16),
            pltpu.VMEM((2, TOKENS, WIDE), BF16),
            pltpu.VMEM((2, 7 * 128, WIDE), BF16),
            pltpu.VMEM((2, 128, WIDE), F32),
            pltpu.VMEM((128, WIDE), F32),
            pltpu.VMEM((128, WIDE), F32),
            pltpu.VMEM((128, 128), F32),
            pltpu.VMEM((16, 8, 128), F32),
            pltpu.VMEM((16, 8, 128), F32),
            pltpu.VMEM((8, 8, WIDE), F32),
            pltpu.SemaphoreType.DMA((3,)), pltpu.SemaphoreType.DMA((2 + 3 * CHUNKS,)),
            *pair(2, CHUNKS, 7),
            *pair(2, CHUNKS),
            *pair(2, CHUNKS),
            *pair(2, CHUNKS, 2),
            *pair(2, CHUNKS, 2),
            *pair(2, CHUNKS),
            *pair(2, CHUNKS, 2),
            *pair(2, CHUNKS, 2),
            *pair(2, CHUNKS, 2),
            *pair(2, CHUNKS, 4),
            *pair(2, CHUNKS, 7),
            *pair(2, CHUNKS),
            *pair(15), *pair(15), *pair(7),
        ],
        compiler_params=pltpu.CompilerParams(collective_id=0, has_side_effects=True, vmem_limit_bytes=63 * 2**20),
    )(inputs, norm_gain, norm_bias, b_up, b_down, d_branch, w_up, w_down.reshape(2, HALF, WIDE))
    return pl.pallas_call(
        last_kernel,
        out_shape=(
            shape((128, WIDE), BF16), shape((128, WIDE), BF16), shape((WIDE, 2 * HALF), BF16), shape((2 * HALF,), F32),
            shape((2 * HALF, WIDE), BF16), shape((WIDE,), F32), shape((WIDE,), F32), shape((WIDE,), F32),
        ),
        in_specs=[hbm] * 8,
        out_specs=(hbm, hbm, hbm, vmem, hbm, hbm, hbm, hbm),
        scratch_shapes=[
            pltpu.VMEM((TOKENS, WIDE), BF16),
            pltpu.VMEM((6, TOKENS, STRIP), BF16),
            pltpu.VMEM((6, WIDE, STRIP), BF16),
            pltpu.VMEM((2 * HALF, WIDE), BF16),
            pltpu.VMEM((128, WIDE), BF16), pltpu.VMEM((128, WIDE), BF16),
            pltpu.VMEM((WIDE,), F32), pltpu.VMEM((WIDE,), F32), pltpu.VMEM((WIDE,), F32),
            pltpu.SemaphoreType.DMA((16,)), pltpu.SemaphoreType.DMA((15,)),
        ],
        compiler_params=pltpu.CompilerParams(vmem_limit_bytes=63 * 2**20),
    )(nrm, gh, grad_w_down, branch, grad_in, grad_gain, grad_bias, grad_b_down)


def solution(mesh):
    placed = (
        P("tensor", "dp"), P("dp"), P("dp"), P("dp", "tensor"), P("tensor"), P("tensor", "dp"), P("dp"), P("tensor", "dp"),
    )
    return jax.shard_map(
        on_device,
        mesh=mesh,
        in_specs=placed,
        out_specs=(
            P("tensor", "dp"), P("tensor", "dp"), P("dp", "tensor"), P("tensor"), P("tensor", "dp"), P("dp"), P("dp"), P("dp"),
        ),
        check_vma=False,
    )
```

```python
import functools

import jax
import jax.numpy as jnp
from jax import lax
from jax.experimental import pallas as pl
from jax.experimental.pallas import tpu as pltpu
from jax.sharding import PartitionSpec as P

MESH = pl.DeviceIdType.MESH
F32, BF16 = jnp.float32, jnp.bfloat16

D = 12288
WIDE = 768
HALF = 1536
TOKENS = 1024
STRIP = 512
K0 = 0.7978845608028654
K1 = 0.044715

OWN = (32, 32, 32, 16, 16)
CHUNKS = len(OWN)
OFF = tuple(sum(OWN[:c]) for c in range(CHUNKS))
SUM_Z = ((0, 2), (0, 3), (1, 2))
GATHER_X = ((0, 0), (0, 3), (1, 3))
T_PAIRS = (1, 2, 3, 4)
R_PAIRS = (0,)
Z_ROWS = tuple(tuple((4 if (k, c) in SUM_Z else 1) * OWN[c] for c in range(CHUNKS)) for k in range(2))
Z_OFF = tuple(tuple(sum(rows[:c]) for c in range(CHUNKS)) for rows in Z_ROWS)

ORDER = (
    ("TZ", 0, 1), ("TY", 0, 0), ("TZ", 0, 3), ("TZ", 0, 2), ("TZ", 0, 4), ("ST", 0, 0), ("TY", 0, 1), ("NM", 0, 0),
    ("TZ", 1, 4), ("TZ", 1, 3), ("TY", 1, 0), ("TZ", 1, 2), ("M", 0, 0), ("TY", 0, 3), ("TY", 0, 2), ("A", 0, 0),
    ("M", 0, 1), ("A", 0, 1), ("TZ", 1, 1), ("B", 0, 0), ("M", 1, 0), ("TY", 1, 3), ("M", 0, 3), ("A", 1, 0),
    ("B", 0, 1), ("A", 0, 3), ("TY", 1, 1), ("TY", 1, 4), ("M", 0, 2), ("M", 1, 3), ("A", 0, 2), ("B", 1, 0),
    ("TY", 1, 2), ("B", 0, 3), ("C", 0, 0), ("A", 1, 3), ("TY", 0, 4), ("M", 1, 1), ("A", 1, 1), ("M", 1, 4),
    ("C", 1, 0), ("C", 0, 1), ("C", 0, 3), ("A", 1, 4), ("M", 1, 2), ("B", 1, 3), ("B", 0, 2), ("M", 0, 4),
    ("A", 0, 4), ("B", 1, 1), ("A", 1, 2), ("C", 0, 2), ("B", 0, 4), ("B", 1, 4), ("C", 1, 3), ("B", 1, 2),
    ("C", 1, 1), ("C", 0, 4), ("G", 0, 0), ("G", 0, 3), ("C", 1, 4), ("G", 0, 1), ("C", 1, 2), ("E1", 0, 0),
    ("E1", 1, 0), ("G", 0, 4), ("E1", 1, 1), ("G", 0, 2), ("E2", 1, 0), ("E2", 0, 0), ("E1", 1, 4), ("E1", 0, 3),
    ("E2", 1, 1), ("E1", 1, 3), ("E3", 1, 0), ("E1", 1, 2), ("F", 1, 0), ("E2", 0, 3), ("E3", 1, 1), ("E2", 1, 4),
    ("E3", 0, 0), ("E2", 1, 3), ("E1", 0, 1), ("F", 0, 0), ("E2", 1, 2), ("E3", 1, 4), ("E3", 0, 3), ("E1", 0, 4),
    ("H1", 1, 0), ("E1", 0, 2), ("F", 1, 4), ("F", 1, 1), ("F", 0, 3), ("E3", 1, 3), ("E3", 1, 2), ("E2", 0, 4),
    ("E2", 0, 1), ("F", 1, 3), ("H1", 0, 0), ("F", 1, 2), ("H", 1, 0), ("E2", 0, 2), ("E3", 0, 4), ("E3", 0, 1),
    ("H", 1, 1), ("F", 0, 4), ("H", 1, 4), ("H", 0, 3), ("H", 1, 3), ("H", 0, 0), ("E3", 0, 2), ("F", 0, 1),
    ("F", 0, 2), ("H", 1, 2), ("S", 0, 0), ("WD", 0, 0), ("WD", 0, 1), ("Z", 0, 0), ("H", 0, 1), ("H", 0, 4),
    ("H", 0, 2),
)


def transposed_dot(left, right):
    return lax.dot_general(left, right, (((1,), (1,)), ((), ())), preferred_element_type=F32)


def dot_transposed(left, right):
    return lax.dot_general(left, right, (((0,), (0,)), ((), ())), preferred_element_type=F32)


def columns_to_rows(first, second):
    lane = lax.broadcasted_iota(jnp.int32, (128, 128), 1)
    return jnp.where(lane == 0, first, jnp.where(lane == 1, second, 0.0)).T[0:8, :]


def rows_to_columns(first, second):
    row = lax.broadcasted_iota(jnp.int32, (128, 128), 0)
    both = jnp.where(row == 0, first, jnp.where(row == 1, second, 0.0)).T
    return both[:, 0:1], both[:, 1:2]


def column_sums(load, width):
    def block(i, total):
        return total + load(pl.ds(pl.multiple_of(i * 16, 16), 16)).astype(F32)

    return jnp.sum(lax.fori_loop(0, TOKENS // 16, block, jnp.zeros((16, width), F32)), axis=0)


def kernel(
    x_hbm, gain_hbm, bias_hbm, b_up_hbm, b_down_hbm, d_hbm, w_up_hbm, w_down_hbm,
    branch_hbm, grad_in_hbm, grad_gain_hbm, grad_bias_hbm, grad_b_up_hbm, grad_b_down_hbm, gw_down_hbm, gh_hbm, nrm_hbm,
    x_ref, gain_ref, bias_ref, b_up_ref, b_down_ref,
    branch_ref, grad_in_ref, grad_gain_ref, grad_bias_ref, grad_b_up_ref, grad_b_down_ref,
    w_up, w_down, dbr, nrm, part, core_in, x1_in, x2_in, z_in, full, t_out, t_in, t_acc,
    standard, grad_normed, inverse_ref, stats, back_stats, gb, b_up_sum,
    load_sem, store_sem, send_sem, recv_sem, small_send, small_recv,
):
    dp, tensor = lax.axis_index("dp"), lax.axis_index("tensor")
    xi, zh, core = dp // 4, (dp // 2) % 2, dp % 2
    yi, zl = tensor // 2, tensor % 2
    x_right, x_left, x_far = (xi + 1) % 4, (xi + 3) % 4, (xi + 2) % 4
    right = (x_right * 4 + zh * 2 + core, tensor)
    left = (x_left * 4 + zh * 2 + core, tensor)
    across = (xi * 4 + (1 - zh) * 2 + core, tensor)
    sibling = (xi * 4 + zh * 2 + (1 - core), tensor)
    t_pair = (dp, yi * 2 + (1 - zl))
    y_to = [(dp, ((yi + dy) % 4) * 2 + zl) for dy in (1, 2, 3)]
    t_to = y_to + [t_pair] + [(dp, ((yi + dy) % 4) * 2 + (1 - zl)) for dy in (1, 2, 3)]
    d_to = []
    for dx in range(4):
        for mz in range(2):
            for mc in range(2):
                if dx or mz or mc:
                    d_to.append((((xi + dx) % 4) * 4 + (1 - zh if mz else zh) * 2 + (1 - core if mc else core), tensor))

    barrier = pltpu.get_barrier_semaphore()
    for device in t_to + d_to:
        pl.semaphore_signal(barrier, inc=1, device_id=device, device_id_type=MESH)

    def rows_at(at, count):
        return pl.ds(pl.multiple_of(at, 16), count)

    pairs = [(d_hbm.at[pl.ds(OFF[c], OWN[c])], dbr.at[rows_at(8 * OFF[c] + tensor * OWN[c], OWN[c])]) for c in range(CHUNKS)]
    pairs += [(x_hbm, x_ref), (gain_hbm, gain_ref), (bias_hbm, bias_ref), (b_up_hbm, b_up_ref), (b_down_hbm, b_down_ref)]
    pairs += [(w_down_hbm, w_down)] + [(w_up_hbm.at[:, pl.ds(h * HALF, HALF)], w_up.at[h]) for h in range(2)]
    loads = [pltpu.make_async_copy(source, target, load_sem.at[i]) for i, (source, target) in enumerate(pairs)]
    for copy in loads:
        copy.start()
    loads = {"d": loads[:CHUNKS], "x": loads[CHUNKS : CHUNKS + 5], 0: loads[CHUNKS + 5 : CHUNKS + 6], 1: loads[CHUNKS + 6 :]}

    def loaded(name):
        for copy in loads.pop(name, ()):
            copy.wait()

    loaded("d")
    pl.semaphore_wait(barrier, len(t_to) + len(d_to))

    kinds = ("t", "tz", "core", "x1", "x2", "z", "ga", "gx", "gf", "gc", "ts", "tr")
    narrow = ("t", "tz", "ts", "tr")
    arriving, leaving = {}, {}

    def send(kind, k, c, source, target, device, rows):
        pltpu.make_async_remote_copy(
            src_ref=source, dst_ref=target, send_sem=send_sem.at[kinds.index(kind), k],
            recv_sem=recv_sem.at[kinds.index(kind), k, c], device_id=device, device_id_type=MESH,
        ).start()
        arriving[kind, k, c] = arriving.get((kind, k, c), 0) + rows
        leaving[kind, k] = leaving.get((kind, k), 0) + rows

    def wait_rows(kind, rows, semaphore):
        place = nrm.at[pl.ds(0, rows)] if kind in narrow else full.at[0, 0, pl.ds(0, rows)]
        pltpu.make_async_copy(place, place, semaphore).wait()

    def arrived(kind, k, c):
        wait_rows(kind, arriving.pop((kind, k, c)), recv_sem.at[kinds.index(kind), k, c])

    def send_small(index, buffer, devices):
        for s, device in enumerate(devices):
            pltpu.make_async_remote_copy(
                src_ref=buffer.at[0], dst_ref=buffer.at[s + 1], send_sem=small_send.at[index],
                recv_sem=small_recv.at[index], device_id=device, device_id_type=MESH,
            ).start()

    def wait_small(semaphore, buffer):
        place = buffer.at[pl.ds(1, buffer.shape[0] - 1)]
        pltpu.make_async_copy(place, place, semaphore).wait()

    stores = []

    def store(source, target):
        copy = pltpu.make_async_copy(source, target, store_sem.at[len(stores)])
        copy.start()
        stores.append(copy)

    tokens = (dbr, nrm)

    def pair_tokens(k, c):
        place = tokens[k].at[rows_at(8 * OFF[c] + tensor * OWN[c], OWN[c])]
        send("tz", k, c, place, place, t_pair, OWN[c])

    def gather_tokens(k, c):
        p = OWN[c]
        if c in T_PAIRS:
            arrived("tz", k, c)
            place = tokens[k].at[rows_at(8 * OFF[c] + yi * 2 * p, 2 * p)]
            for device in y_to:
                send("t", k, c, place, place, device, 2 * p)
        else:
            place = tokens[k].at[rows_at(8 * OFF[c] + tensor * p, p)]
            for device in t_to:
                send("t", k, c, place, place, device, p)

    def statistics(k, c):
        loaded("x")
        widened = x_ref[...].astype(F32)
        total = jnp.sum(widened, axis=1, keepdims=True)
        off = widened - total / WIDE
        stats[0] = columns_to_rows(total, jnp.sum(off * off, axis=1, keepdims=True))
        send_small(0, stats, d_to)

    def normalise(k, c):
        wait_small(small_recv.at[0], stats)
        sums = [stats[s, 0:1, :] for s in range(16)]
        mean = functools.reduce(jnp.add, sums) / D
        spread = jnp.zeros_like(mean)
        for s in range(16):
            apart = sums[s] / WIDE - mean
            spread = spread + (stats[s, 1:2, :] + WIDE * (apart * apart))
        mean, inverse = rows_to_columns(mean, lax.rsqrt(spread / D + 1e-05))
        inverse_ref[...] = jnp.broadcast_to(inverse, (128, 128))
        gain, bias = gain_ref[...].reshape(1, WIDE), bias_ref[...].reshape(1, WIDE)
        for c in range(CHUNKS):
            rows = slice(OFF[c], OFF[c] + OWN[c])
            std = (x_ref[rows, :].astype(F32) - mean[rows]) * inverse[rows]
            standard[rows, :] = std
            nrm[rows_at(8 * OFF[c] + tensor * OWN[c], OWN[c]), :] = (std * gain + bias).astype(BF16)

    def accumulate(k, c, start, count, others, columns=slice(None)):
        size = 32 if count % 32 == 0 else 16

        def block(i, _):
            at = i * size
            rows = rows_at(8 * OFF[c] + start + at, size)
            value = part[k, core, rows, columns].astype(F32)
            for load in others:
                value = value + load(at, size).astype(F32)
            part[k, core, rows, columns] = value.astype(BF16)
            return 0

        if count == size:
            block(0, 0)
        else:
            lax.fori_loop(0, count // size, block, 0)

    def multiply(k, c):
        loaded(k)
        arrived("t", k, c)
        rows = pl.ds(8 * OFF[c], 8 * OWN[c])

        def one(step, _):
            half = (1 - core) * (1 - step) + core * step
            if k:
                value = jnp.dot(nrm[rows, :], w_up[half], preferred_element_type=F32)
            else:
                value = transposed_dot(dbr[rows, :], w_down[half])
            part[k, half, rows, :] = value.astype(BF16)

            @pl.when(step == 0)
            def _():
                send("core", k, c, part.at[k, 1 - core, rows], core_in.at[k, rows], sibling, 8 * OWN[c])

            return 0

        lax.fori_loop(0, 2, one, 0)

    def part_rows(k, c, start, count):
        return part.at[k, core, rows_at(8 * OFF[c] + start, count)]

    def half_columns(side):
        return pl.ds(side * WIDE, WIDE)

    def add_core(k, c):
        p = OWN[c]
        arrived("core", k, c)

        def add(start, count):
            accumulate(k, c, start, count, [lambda at, size: core_in[k, rows_at(8 * OFF[c] + start + at, size), :]])

        if (k, c) in SUM_Z:
            for x in range(4):
                start = (2 * x + 1 - zh) * p
                add(start, p)
                send("z", k, c, part_rows(k, c, start, p), z_in.at[k, pl.ds(Z_OFF[k][c] + x * p, p)], across, p)
            for x in range(4):
                add((2 * x + zh) * p, p)
        else:
            add(x_far * 2 * p, 2 * p)
            for side, device in enumerate((right, left)):
                source = part_rows(k, c, x_far * 2 * p + side * p, p)
                send("x1", k, c, source, x1_in.at[k, side, pl.ds(OFF[c], p)], device, p)
            for piece in (x_right, x_left, xi):
                add(piece * 2 * p, 2 * p)

    def add_first(k, c):
        p = OWN[c]
        sides = ((x_right, right), (x_left, left))
        if (k, c) in SUM_Z:
            arrived("z", k, c)

            def add(piece):
                accumulate(
                    k, c, (2 * piece + zh) * p, p, [lambda at, size: z_in[k, rows_at(Z_OFF[k][c] + piece * p + at, size), :]]
                )

            add(x_far)
            far = part_rows(k, c, (2 * x_far + zh) * p, p)
            for side, (_, device) in enumerate(sides):
                target = x1_in.at[k, side, pl.ds(OFF[c], p), half_columns(side)]
                send("x1", k, c, far.at[:, half_columns(side)], target, device, p // 2)
            for piece in (x_right, x_left, xi):
                add(piece)
        else:
            arrived("x1", k, c)
            for side, (piece, device) in enumerate(sides):
                accumulate(
                    k, c, piece * 2 * p + side * p, p, [lambda at, size: x1_in[k, side, rows_at(OFF[c] + at, size), :]]
                )
                source = part_rows(k, c, piece * 2 * p, 2 * p)
                send("x2", k, c, source, x2_in.at[k, side, pl.ds(2 * OFF[c], 2 * p)], device, 2 * p)

    def add_second(k, c):
        p = OWN[c]
        if (k, c) in SUM_Z:
            arrived("x1", k, c)
            for side, (piece, device) in enumerate(((x_right, right), (x_left, left))):
                columns = half_columns(side)
                accumulate(
                    k, c, (2 * piece + zh) * p, p, [lambda at, size: x1_in[k, side, rows_at(OFF[c] + at, size), columns]], columns
                )
                source = part_rows(k, c, (2 * piece + zh) * p, p)
                send("x2", k, c, source, x2_in.at[k, side, pl.ds(2 * OFF[c], p)], device, p)
            return
        arrived("x2", k, c)

        def add(sub):
            start = sub * p
            accumulate(
                k, c, xi * 2 * p + start, p,
                [lambda at, size, side=side: x2_in[k, side, rows_at(2 * OFF[c] + start + at, size), :] for side in range(2)],
            )

        add(1 - zh)
        source = part_rows(k, c, xi * 2 * p + (1 - zh) * p, p)
        send("z", k, c, source, z_in.at[k, pl.ds(Z_OFF[k][c], p)], across, p)
        add(zh)

    def activate(_, c):
        p = OWN[c]
        mine = (2 * xi + zh) * p
        for k in range(2):
            arrived("x2" if (k, c) in SUM_Z else "z", k, c)
        bias = b_up_ref[pl.ds(pl.multiple_of(core * HALF, HALF), HALF)].reshape(1, HALF)

        def total(k, at):
            value = part[k, core, rows_at(8 * OFF[c] + mine + at, 16), :].astype(F32)
            if (k, c) in SUM_Z:
                for side in range(2):
                    value = value + x2_in[k, side, rows_at(2 * OFF[c] + at, 16), :].astype(F32)
                return value
            return value + z_in[k, rows_at(Z_OFF[k][c] + at, 16), :].astype(F32)

        def block(i, _):
            at = i * 16
            rows = rows_at(8 * OFF[c] + mine + at, 16)
            h = total(1, at) + bias
            square = h * h
            t = jnp.tanh(K0 * (h + K1 * (square * h)))
            full[0, core, rows, :] = (0.5 * h * (1.0 + t)).astype(BF16)
            slope = 0.5 * (1.0 + t) + 0.5 * h * (1.0 - t * t) * (K0 * (1.0 + 3.0 * K1 * square))
            full[1, core, rows, :] = (total(0, at) * slope).astype(BF16)
            return 0

        lax.fori_loop(0, p // 16, block, 0)
        for k in (1, 0):
            place = full.at[k, core, rows_at(8 * OFF[c] + mine, p)]
            for device in (right, left) if (k, c) in GATHER_X else (across,):
                send("ga", k, c, place, place, device, p)

    def full_rows(k, c, start, count):
        return full.at[k, core, rows_at(8 * OFF[c] + start, count)]

    def pass_on(kind, k, c, start, count, device):
        place = full_rows(k, c, start, count)
        send(kind, k, c, place, place, device, count)

    def gather_first(k, c):
        p = OWN[c]
        arrived("ga", k, c)
        if (k, c) in GATHER_X:
            for side, (piece, device) in enumerate(((x_left, right), (x_right, left))):
                place = full_rows(k, c, (2 * piece + zh) * p, p).at[:, half_columns(side)]
                send("gf", k, c, place, place, device, p // 2)
        else:
            for device in (right, left):
                pass_on("gx", k, c, xi * 2 * p, 2 * p, device)
            pass_on("gc", k, c, xi * 2 * p, 2 * p, sibling)

    def gather_second(k, c):
        p = OWN[c]
        if (k, c) in GATHER_X:
            arrived("gf", k, c)
            for x in range(4):
                pass_on("gx", k, c, (2 * x + zh) * p, p, across)
            for x in range(4):
                pass_on("gc", k, c, (2 * x + zh) * p, p, sibling)
        else:
            arrived("gx", k, c)
            for side, (piece, device) in enumerate(((x_left, right), (x_right, left))):
                pass_on("gf", k, c, piece * 2 * p + side * p, p, device)
            for piece in (x_left, x_right):
                pass_on("gc", k, c, piece * 2 * p, 2 * p, sibling)

    def gather_third(k, c):
        p = OWN[c]
        if (k, c) in GATHER_X:
            arrived("gx", k, c)
            for x in range(4):
                pass_on("gc", k, c, (2 * x + 1 - zh) * p, p, sibling)
        else:
            arrived("gf", k, c)
            pass_on("gc", k, c, x_far * 2 * p, 2 * p, sibling)

    def multiply_back(k, c):
        p = OWN[c]
        arrived("gc", k, c)
        rows = pl.ds(8 * OFF[c], 8 * p)

        def tile(j, _):
            at = pl.ds(pl.multiple_of(j * 256, 256), 256)
            if k:
                value = transposed_dot(full[1, 0, rows, :], w_up[0, at, :])
                value += transposed_dot(full[1, 1, rows, :], w_up[1, at, :])
            else:
                value = jnp.dot(full[0, 0, rows, :], w_down[0, :, at], preferred_element_type=F32)
                value += jnp.dot(full[0, 1, rows, :], w_down[1, :, at], preferred_element_type=F32)
            t_out[k, rows, at] = value.astype(BF16)
            return 0

        lax.fori_loop(0, WIDE // 256, tile, 0)
        if k:
            for half in range(2):
                store(full.at[1, half, rows], gh_hbm.at[rows, pl.ds(half * HALF, HALF)])
            store(nrm.at[rows], nrm_hbm.at[rows])
        if c in R_PAIRS:
            for s, device in enumerate(y_to):
                place = t_out.at[k, rows_at(8 * OFF[c] + (device[1] // 2) * 2 * p, 2 * p)]
                send("ts", k, c, place, t_in.at[k, pl.ds(7 * OFF[c] + s * 2 * p, 2 * p)], device, 2 * p)
        else:
            for s, device in enumerate(t_to):
                place = t_out.at[k, rows_at(8 * OFF[c] + device[1] * p, p)]
                send("ts", k, c, place, t_in.at[k, pl.ds(7 * OFF[c] + s * p, p)], device, p)
        if k:
            for half in range(2):

                def block(i, total):
                    return total + full[1, half, pl.ds(pl.multiple_of(8 * OFF[c] + i * 16, 16), 16), :].astype(F32)

                b_up_sum[half] = lax.fori_loop(0, p // 2, block, b_up_sum[half])

    def halve_tokens(k, c):
        p = OWN[c]
        arrived("ts", k, c)

        def total(sub):
            value = t_out[k, rows_at(8 * OFF[c] + (yi * 2 + sub) * p, p), :].astype(F32)
            for s in range(3):
                value = value + t_in[k, rows_at(7 * OFF[c] + s * 2 * p + sub * p, p), :].astype(F32)
            return value

        place = rows_at(8 * OFF[c] + (yi * 2 + 1 - zl) * p, p)
        t_out[k, place, :] = total(1 - zl).astype(BF16)
        send("tr", k, c, t_out.at[k, place], t_in.at[k, pl.ds(7 * OFF[c] + 6 * p, p)], t_pair, p)
        t_acc[k, OFF[c] : OFF[c] + p, :] = total(zl)

    def finish_tokens(k, c):
        p = OWN[c]
        rows = slice(OFF[c], OFF[c] + p)
        if c in R_PAIRS:
            arrived("tr", k, c)
            value = t_acc[k, rows, :] + t_in[k, 7 * OFF[c] + 6 * p : 7 * OFF[c] + 7 * p, :].astype(F32)
        else:
            arrived("ts", k, c)
            value = t_out[k, rows_at(8 * OFF[c] + tensor * p, p), :].astype(F32)
            for s in range(7):
                value = value + t_in[k, 7 * OFF[c] + s * p : 7 * OFF[c] + (s + 1) * p, :].astype(F32)
        if k:
            grad_normed[rows, :] = value
        else:
            branch_ref[rows, :] = (value + b_down_ref[...].reshape(1, WIDE)).astype(BF16)

    def weight_down(_, half):
        def strip(i, _):
            at = pl.ds(pl.multiple_of(i * STRIP, STRIP), STRIP)
            w_down[half, at, :] = dot_transposed(full[0, half, :, at], dbr[...]).astype(BF16)
            return 0

        lax.fori_loop(0, HALF // STRIP, strip, 0)
        store(w_down.at[half], gw_down_hbm.at[pl.ds(half * HALF, HALF)])
        if half == 0:
            grad_b_down_ref[...] = column_sums(lambda rows: dbr[rows, :], WIDE)

    def back_sums(k, c):
        gn, std = grad_normed[...], standard[...]
        scaled = gn * gain_ref[...].reshape(1, WIDE)
        back_stats[0] = columns_to_rows(
            jnp.sum(scaled, axis=1, keepdims=True), jnp.sum(scaled * std, axis=1, keepdims=True)
        )
        send_small(1, back_stats, d_to)
        gb[0, 0:1, :] = jnp.sum(gn * std, axis=0, keepdims=True)
        gb[0, 1:2, :] = jnp.sum(gn, axis=0, keepdims=True)
        gb[0, 2:8, :] = jnp.zeros((6, WIDE), F32)
        send_small(2, gb, t_to)

    def grad_inputs(k, c):
        wait_small(small_recv.at[1], back_stats)
        first = functools.reduce(jnp.add, [back_stats[s, 0:1, :] for s in range(16)]) / D
        second = functools.reduce(jnp.add, [back_stats[s, 1:2, :] for s in range(16)]) / D
        first, second = rows_to_columns(first, second)
        scaled = grad_normed[...] * gain_ref[...].reshape(1, WIDE)
        grad_in_ref[...] = (inverse_ref[:, 0:1] * (scaled - first - standard[...] * second)).astype(BF16)
        wait_small(small_recv.at[2], gb)
        both = functools.reduce(jnp.add, [gb[s] for s in range(8)])
        grad_gain_ref[...] = both[0]
        grad_bias_ref[...] = both[1]
        for half in range(2):
            grad_b_up_ref[half * HALF : (half + 1) * HALF] = jnp.sum(b_up_sum[half], axis=0)

    steps = {
        "TZ": pair_tokens, "TY": gather_tokens, "ST": statistics, "NM": normalise, "M": multiply, "A": add_core,
        "B": add_first, "C": add_second, "G": activate, "E1": gather_first, "E2": gather_second, "E3": gather_third,
        "F": multiply_back, "H1": halve_tokens, "H": finish_tokens, "WD": weight_down,
        "S": back_sums, "Z": grad_inputs,
    }
    b_up_sum[...] = jnp.zeros_like(b_up_sum)
    for name, k, c in ORDER:
        steps[name](k, c)
    for source, target in (
        (branch_ref, branch_hbm), (grad_in_ref, grad_in_hbm), (grad_gain_ref, grad_gain_hbm), (grad_bias_ref, grad_bias_hbm),
        (grad_b_up_ref, grad_b_up_hbm), (grad_b_down_ref, grad_b_down_hbm),
    ):
        store(source, target)
    for (kind, k), rows in leaving.items():
        wait_rows(kind, rows, send_sem.at[kinds.index(kind), k])
    for index, buffer in enumerate((stats, back_stats, gb)):
        wait_small(small_send.at[index], buffer)
    for copy in stores:
        copy.wait()


def last_kernel(
    nrm_hbm, gh_hbm, gw_down_hbm, branch_in, grad_in_in, gain_in, bias_in, b_up_in, b_down_in,
    branch_out, grad_in_out, gw_up_out, b_up_out, gw_down_out, b_down_out, gain_out, bias_out,
    nrm, gh, gw_up, gw_down, branch, grad_in, gain, bias, b_up, b_down, in_sem, out_sem,
):
    strips, parts = 2 * HALF // STRIP, 4

    def columns(i):
        return pl.ds(i * STRIP, STRIP)

    ins, outs = [], []

    def fetch(source, target):
        copy = pltpu.make_async_copy(source, target, in_sem.at[len(ins)])
        copy.start()
        ins.append(copy)
        return copy

    def put(source, target):
        copy = pltpu.make_async_copy(source, target, out_sem.at[len(outs)])
        copy.start()
        outs.append(copy)

    first = fetch(nrm_hbm, nrm)
    strip_in = [fetch(gh_hbm.at[:, columns(i)], gh.at[i]) for i in range(strips)]
    rows = [pl.ds(i * (2 * HALF // parts), 2 * HALF // parts) for i in range(parts)]
    passing = [(fetch(gw_down_hbm.at[r], gw_down.at[r]), gw_down.at[r], gw_down_out.at[r]) for r in rows]
    for source, held, target in (
        (branch_in, branch, branch_out), (grad_in_in, grad_in, grad_in_out), (gain_in, gain, gain_out),
        (bias_in, bias, bias_out), (b_up_in, b_up, b_up_out), (b_down_in, b_down, b_down_out),
    ):
        passing.append((fetch(source, held), held, target))
    first.wait()
    for i in range(strips):
        strip_in[i].wait()
        gw_up[i] = dot_transposed(nrm[...], gh[i]).astype(BF16)
        put(gw_up.at[i], gw_up_out.at[:, columns(i)])
        if i >= 2:
            for copy, held, target in passing[(i - 2) * 3 : (i - 1) * 3]:
                copy.wait()
                put(held, target)
    for copy in outs:
        copy.wait()


def on_device(inputs, norm_gain, norm_bias, w_up, b_up, w_down, b_down, d_branch):
    hbm = pl.BlockSpec(memory_space=pl.ANY)
    shape = jax.ShapeDtypeStruct

    dma = pltpu.SemaphoreType.DMA

    branch, grad_in, grad_gain, grad_bias, grad_b_up, grad_b_down, grad_w_down, gh, nrm = pl.pallas_call(
        kernel,
        out_shape=(
            shape((128, WIDE), BF16), shape((128, WIDE), BF16), shape((WIDE,), F32), shape((WIDE,), F32), shape((2 * HALF,), F32),
            shape((WIDE,), F32), shape((2 * HALF, WIDE), BF16), shape((TOKENS, 2 * HALF), BF16), shape((TOKENS, WIDE), BF16),
        ),
        in_specs=[hbm] * 8,
        out_specs=(hbm,) * 9,
        scratch_shapes=[
            pltpu.VMEM((128, WIDE), BF16),
            pltpu.VMEM((WIDE,), F32), pltpu.VMEM((WIDE,), F32), pltpu.VMEM((2 * HALF,), F32), pltpu.VMEM((WIDE,), F32),
            pltpu.VMEM((128, WIDE), BF16), pltpu.VMEM((128, WIDE), BF16),
            pltpu.VMEM((WIDE,), F32), pltpu.VMEM((WIDE,), F32), pltpu.VMEM((2 * HALF,), F32), pltpu.VMEM((WIDE,), F32),
            pltpu.VMEM((2, WIDE, HALF), BF16),
            pltpu.VMEM((2, HALF, WIDE), BF16),
            pltpu.VMEM((TOKENS, WIDE), BF16),
            pltpu.VMEM((TOKENS, WIDE), BF16),
            pltpu.VMEM((2, 2, TOKENS, HALF), BF16),
            pltpu.VMEM((2, TOKENS, HALF), BF16),
            pltpu.VMEM((2, 2, 128, HALF), BF16),
            pltpu.VMEM((2, 2, 256, HALF), BF16),
            pltpu.VMEM((2, max(sum(rows) for rows in Z_ROWS), HALF), BF16),
            pltpu.VMEM((2, 2, TOKENS, HALF), BF16),
            pltpu.VMEM((2, TOKENS, WIDE), BF16),
            pltpu.VMEM((2, 7 * 128, WIDE), BF16),
            pltpu.VMEM((2, 128, WIDE), F32),
            pltpu.VMEM((128, WIDE), F32),
            pltpu.VMEM((128, WIDE), F32),
            pltpu.VMEM((128, 128), F32),
            pltpu.VMEM((16, 8, 128), F32),
            pltpu.VMEM((16, 8, 128), F32),
            pltpu.VMEM((8, 8, WIDE), F32),
            pltpu.VMEM((2, 16, HALF), F32),
            dma((CHUNKS + 8,)), dma((8 + 3 * CHUNKS,)), dma((12, 2)), dma((12, 2, CHUNKS)), dma((3,)), dma((3,)),
        ],
        compiler_params=pltpu.CompilerParams(collective_id=0, has_side_effects=True, vmem_limit_bytes=63 * 2**20),
    )(inputs, norm_gain, norm_bias, b_up, b_down, d_branch, w_up, w_down.reshape(2, HALF, WIDE))
    return pl.pallas_call(
        last_kernel,
        out_shape=(
            shape((128, WIDE), BF16), shape((128, WIDE), BF16), shape((WIDE, 2 * HALF), BF16), shape((2 * HALF,), F32),
            shape((2 * HALF, WIDE), BF16), shape((WIDE,), F32), shape((WIDE,), F32), shape((WIDE,), F32),
        ),
        in_specs=[hbm] * 9,
        out_specs=(hbm,) * 8,
        scratch_shapes=[
            pltpu.VMEM((TOKENS, WIDE), BF16),
            pltpu.VMEM((6, TOKENS, STRIP), BF16),
            pltpu.VMEM((6, WIDE, STRIP), BF16),
            pltpu.VMEM((2 * HALF, WIDE), BF16),
            pltpu.VMEM((128, WIDE), BF16), pltpu.VMEM((128, WIDE), BF16),
            pltpu.VMEM((WIDE,), F32), pltpu.VMEM((WIDE,), F32), pltpu.VMEM((2 * HALF,), F32), pltpu.VMEM((WIDE,), F32),
            dma((17,)), dma((16,)),
        ],
        compiler_params=pltpu.CompilerParams(vmem_limit_bytes=63 * 2**20),
    )(nrm, gh, grad_w_down, branch, grad_in, grad_gain, grad_bias, grad_b_up, grad_b_down)


def solution(mesh):
    placed = (
        P("tensor", "dp"), P("dp"), P("dp"), P("dp", "tensor"), P("tensor"), P("tensor", "dp"), P("dp"), P("tensor", "dp"),
    )
    return jax.shard_map(
        on_device,
        mesh=mesh,
        in_specs=placed,
        out_specs=(
            P("tensor", "dp"), P("tensor", "dp"), P("dp", "tensor"), P("tensor"), P("tensor", "dp"), P("dp"), P("dp"), P("dp"),
        ),
        check_vma=False,
    )
```

```python
import functools

import jax
import jax.numpy as jnp
from jax import lax
from jax.experimental import pallas as pl
from jax.experimental.pallas import tpu as pltpu
from jax.sharding import PartitionSpec as P

MESH = pl.DeviceIdType.MESH
F32, BF16 = jnp.float32, jnp.bfloat16

D = 12288
WIDE = 768
HALF = 1536
TOKENS = 1024
STRIP = 512
K0 = 0.7978845608028654
K1 = 0.044715

OWN = (32, 32, 16, 16, 16, 16)
CHUNKS = len(OWN)
OFF = tuple(sum(OWN[:c]) for c in range(CHUNKS))
SUM_Z = ((0, 2), (0, 5), (1, 3), (1, 4), (1, 5))
GATHER_X = ((0, 0), (0, 2), (1, 3), (1, 5))
T_PAIRS = (1, 2, 3, 4, 5)
R_PAIRS = (0, 2)
Z_ROWS = tuple(tuple((4 if (k, c) in SUM_Z else 1) * OWN[c] for c in range(CHUNKS)) for k in range(2))
Z_OFF = tuple(tuple(sum(rows[:c]) for c in range(CHUNKS)) for rows in Z_ROWS)

ORDER = (
    ("TZ", 0, 2), ("TZ", 0, 3), ("TY", 0, 0), ("ST", 0, 0), ("TZ", 0, 4), ("TZ", 0, 1), ("TY", 0, 2), ("NM", 0, 0),
    ("TZ", 1, 3), ("TY", 0, 3), ("TZ", 1, 2), ("TZ", 0, 5), ("TZ", 1, 5), ("TZ", 1, 4), ("TY", 1, 0), ("M", 0, 0),
    ("TY", 1, 3), ("TZ", 1, 1), ("TY", 1, 2), ("A", 0, 0), ("M", 0, 2), ("M", 0, 3), ("TY", 0, 5), ("B", 0, 0),
    ("A", 0, 2), ("M", 1, 0), ("TY", 0, 1), ("TY", 1, 4), ("A", 0, 3), ("A", 1, 0), ("M", 1, 3), ("TY", 1, 5),
    ("B", 0, 2), ("C", 0, 0), ("B", 0, 3), ("M", 0, 5), ("B", 1, 0), ("A", 1, 3), ("A", 0, 5), ("TY", 0, 4),
    ("C", 0, 2), ("M", 1, 2), ("M", 0, 1), ("TY", 1, 1), ("A", 1, 2), ("A", 0, 1), ("M", 1, 5), ("B", 1, 3),
    ("C", 1, 0), ("C", 0, 3), ("B", 1, 2), ("A", 1, 5), ("B", 0, 1), ("C", 1, 3), ("M", 1, 4), ("C", 1, 2),
    ("M", 1, 1), ("G", 0, 0), ("A", 1, 4), ("A", 1, 1), ("B", 0, 5), ("C", 0, 1), ("M", 0, 4), ("E1", 0, 0),
    ("B", 1, 5), ("A", 0, 4), ("B", 1, 1), ("C", 1, 5), ("G", 0, 3), ("E2", 0, 0), ("C", 0, 5), ("B", 1, 4),
    ("E1", 1, 0), ("C", 1, 1), ("G", 0, 2), ("B", 0, 4), ("C", 1, 4), ("G", 0, 5), ("E3", 0, 0), ("G", 0, 1),
    ("E1", 0, 2), ("E2", 1, 0), ("F", 0, 0), ("E1", 1, 2), ("C", 0, 4), ("E1", 0, 5), ("E1", 1, 3), ("E1", 1, 5),
    ("E2", 0, 2), ("E3", 1, 0), ("E2", 1, 2), ("E1", 1, 1), ("G", 0, 4), ("F", 1, 0), ("E2", 1, 3), ("E3", 1, 2),
    ("E3", 0, 2), ("E2", 1, 5), ("E2", 0, 5), ("E1", 1, 4), ("F", 1, 2), ("E1", 0, 3), ("F", 0, 2), ("E2", 1, 1),
    ("E3", 0, 5), ("E1", 0, 4), ("E3", 1, 3), ("F", 0, 5), ("F", 1, 3), ("H1", 0, 0), ("E2", 1, 4), ("H1", 1, 0),
    ("E3", 1, 5), ("H1", 1, 2), ("E3", 1, 1), ("E1", 0, 1), ("F", 1, 5), ("H1", 0, 2), ("F", 1, 1), ("E2", 0, 3),
    ("E3", 1, 4), ("H", 1, 0), ("E2", 0, 4), ("E2", 0, 1), ("H", 1, 3), ("F", 1, 4), ("H", 0, 0), ("E3", 0, 3),
    ("H", 0, 2), ("E3", 0, 4), ("H", 0, 5), ("H", 1, 2), ("H", 1, 5), ("F", 0, 3), ("E3", 0, 1), ("F", 0, 4),
    ("F", 0, 1), ("WD", 0, 1), ("H", 1, 4), ("H", 1, 1), ("S", 0, 0), ("H", 0, 3), ("WD", 0, 0), ("Z", 0, 0),
    ("H", 0, 1), ("H", 0, 4),
)


def transposed_dot(left, right):
    return lax.dot_general(left, right, (((1,), (1,)), ((), ())), preferred_element_type=F32)


def dot_transposed(left, right):
    return lax.dot_general(left, right, (((0,), (0,)), ((), ())), preferred_element_type=F32)


def columns_to_rows(first, second):
    lane = lax.broadcasted_iota(jnp.int32, (128, 128), 1)
    return jnp.where(lane == 0, first, jnp.where(lane == 1, second, 0.0)).T[0:8, :]


def rows_to_columns(first, second):
    row = lax.broadcasted_iota(jnp.int32, (128, 128), 0)
    both = jnp.where(row == 0, first, jnp.where(row == 1, second, 0.0)).T
    return both[:, 0:1], both[:, 1:2]


def kernel(
    x_hbm, gain_hbm, bias_hbm, b_up_hbm, b_down_hbm, d_hbm, w_up_hbm, w_down_hbm,
    branch_hbm, grad_in_hbm, grad_gain_hbm, grad_bias_hbm, grad_b_up_hbm, grad_b_down_hbm, gw_down_hbm, gh_hbm, nrm_hbm,
    x_ref, gain_ref, bias_ref, b_up_ref, b_down_ref,
    branch_ref, grad_in_ref, grad_gain_ref, grad_bias_ref, grad_b_up_ref, grad_b_down_ref,
    w_up, w_down, dbr, nrm, part, core_in, x1_in, x2_in, z_in, full, t_out, t_in, t_acc,
    standard, grad_normed, inverse_ref, stats, back_stats, gb, b_up_sum, b_down_sum,
    load_sem, store_sem, strip_sem, send_sem, recv_sem, small_send, small_recv,
):
    dp, tensor = lax.axis_index("dp"), lax.axis_index("tensor")
    xi, zh, core = dp // 4, (dp // 2) % 2, dp % 2
    yi, zl = tensor // 2, tensor % 2
    x_right, x_left, x_far = (xi + 1) % 4, (xi + 3) % 4, (xi + 2) % 4
    right = (x_right * 4 + zh * 2 + core, tensor)
    left = (x_left * 4 + zh * 2 + core, tensor)
    across = (xi * 4 + (1 - zh) * 2 + core, tensor)
    sibling = (xi * 4 + zh * 2 + (1 - core), tensor)
    t_pair = (dp, yi * 2 + (1 - zl))
    y_to = [(dp, ((yi + dy) % 4) * 2 + zl) for dy in (1, 2, 3)]
    t_to = y_to + [t_pair] + [(dp, ((yi + dy) % 4) * 2 + (1 - zl)) for dy in (1, 2, 3)]
    d_to = []
    for dx in range(4):
        for mz in range(2):
            for mc in range(2):
                if dx or mz or mc:
                    d_to.append((((xi + dx) % 4) * 4 + (1 - zh if mz else zh) * 2 + (1 - core if mc else core), tensor))

    barrier = pltpu.get_barrier_semaphore()
    for device in t_to + d_to:
        pl.semaphore_signal(barrier, inc=1, device_id=device, device_id_type=MESH)

    def rows_at(at, count):
        return pl.ds(pl.multiple_of(at, 16), count)

    pairs = [(d_hbm.at[pl.ds(OFF[c], OWN[c])], dbr.at[rows_at(8 * OFF[c] + tensor * OWN[c], OWN[c])]) for c in range(CHUNKS)]
    pairs += [(x_hbm, x_ref), (gain_hbm, gain_ref), (bias_hbm, bias_ref), (b_up_hbm, b_up_ref), (b_down_hbm, b_down_ref)]
    pairs += [(w_down_hbm, w_down)] + [(w_up_hbm.at[:, pl.ds(h * HALF, HALF)], w_up.at[h]) for h in range(2)]
    loads = [pltpu.make_async_copy(source, target, load_sem.at[i]) for i, (source, target) in enumerate(pairs)]
    for copy in loads:
        copy.start()
    loads = {"d": loads[:CHUNKS], "x": loads[CHUNKS : CHUNKS + 5], 0: loads[CHUNKS + 5 : CHUNKS + 6], 1: loads[CHUNKS + 6 :]}

    def loaded(name):
        for copy in loads.pop(name, ()):
            copy.wait()

    loaded("d")
    pl.semaphore_wait(barrier, len(t_to) + len(d_to))

    kinds = ("t", "tz", "core", "x1", "x2", "z", "ga", "gx", "gf", "gc", "ts", "tr")
    narrow = ("t", "tz", "ts", "tr")
    arriving, leaving = {}, {}

    def send(kind, k, c, source, target, device, rows):
        pltpu.make_async_remote_copy(
            src_ref=source, dst_ref=target, send_sem=send_sem.at[kinds.index(kind), k],
            recv_sem=recv_sem.at[kinds.index(kind), k, c], device_id=device, device_id_type=MESH,
        ).start()
        arriving[kind, k, c] = arriving.get((kind, k, c), 0) + rows
        leaving[kind, k] = leaving.get((kind, k), 0) + rows

    def wait_rows(kind, rows, semaphore):
        place = nrm.at[pl.ds(0, rows)] if kind in narrow else full.at[0, 0, pl.ds(0, rows)]
        pltpu.make_async_copy(place, place, semaphore).wait()

    def arrived(kind, k, c):
        wait_rows(kind, arriving.pop((kind, k, c)), recv_sem.at[kinds.index(kind), k, c])

    def send_small(index, buffer, devices):
        for s, device in enumerate(devices):
            pltpu.make_async_remote_copy(
                src_ref=buffer.at[0], dst_ref=buffer.at[s + 1], send_sem=small_send.at[index],
                recv_sem=small_recv.at[index], device_id=device, device_id_type=MESH,
            ).start()

    def wait_small(semaphore, buffer):
        place = buffer.at[pl.ds(1, buffer.shape[0] - 1)]
        pltpu.make_async_copy(place, place, semaphore).wait()

    stores = []

    def store(source, target):
        copy = pltpu.make_async_copy(source, target, store_sem.at[len(stores)])
        copy.start()
        stores.append(copy)

    tokens = (dbr, nrm)

    def pair_tokens(k, c):
        place = tokens[k].at[rows_at(8 * OFF[c] + tensor * OWN[c], OWN[c])]
        send("tz", k, c, place, place, t_pair, OWN[c])

    def gather_tokens(k, c):
        p = OWN[c]
        if c in T_PAIRS:
            arrived("tz", k, c)
            place = tokens[k].at[rows_at(8 * OFF[c] + yi * 2 * p, 2 * p)]
            for device in y_to:
                send("t", k, c, place, place, device, 2 * p)
        else:
            place = tokens[k].at[rows_at(8 * OFF[c] + tensor * p, p)]
            for device in t_to:
                send("t", k, c, place, place, device, p)

    def statistics(k, c):
        loaded("x")
        widened = x_ref[...].astype(F32)
        total = jnp.sum(widened, axis=1, keepdims=True)
        off = widened - total / WIDE
        stats[0] = columns_to_rows(total, jnp.sum(off * off, axis=1, keepdims=True))
        send_small(0, stats, d_to)

    def normalise(k, c):
        wait_small(small_recv.at[0], stats)
        sums = [stats[s, 0:1, :] for s in range(16)]
        mean = functools.reduce(jnp.add, sums) / D
        spread = jnp.zeros_like(mean)
        for s in range(16):
            apart = sums[s] / WIDE - mean
            spread = spread + (stats[s, 1:2, :] + WIDE * (apart * apart))
        mean, inverse = rows_to_columns(mean, lax.rsqrt(spread / D + 1e-05))
        inverse_ref[...] = jnp.broadcast_to(inverse, (128, 128))
        gain, bias = gain_ref[...].reshape(1, WIDE), bias_ref[...].reshape(1, WIDE)
        for c in range(CHUNKS):
            rows = slice(OFF[c], OFF[c] + OWN[c])
            std = (x_ref[rows, :].astype(F32) - mean[rows]) * inverse[rows]
            standard[rows, :] = std
            nrm[rows_at(8 * OFF[c] + tensor * OWN[c], OWN[c]), :] = (std * gain + bias).astype(BF16)

    def accumulate(k, c, start, count, others, columns=slice(None)):
        size = 32 if count % 32 == 0 else 16

        def block(i, _):
            at = i * size
            rows = rows_at(8 * OFF[c] + start + at, size)
            value = part[k, core, rows, columns].astype(F32)
            for load in others:
                value = value + load(at, size).astype(F32)
            part[k, core, rows, columns] = value.astype(BF16)
            return 0

        if count == size:
            block(0, 0)
        else:
            lax.fori_loop(0, count // size, block, 0)

    def multiply(k, c):
        loaded(k)
        arrived("t", k, c)
        rows = pl.ds(8 * OFF[c], 8 * OWN[c])

        def one(step, _):
            half = (1 - core) * (1 - step) + core * step
            if k:
                value = jnp.dot(nrm[rows, :], w_up[half], preferred_element_type=F32)
            else:
                value = transposed_dot(dbr[rows, :], w_down[half])
            part[k, half, rows, :] = value.astype(BF16)

            @pl.when(step == 0)
            def _():
                send("core", k, c, part.at[k, 1 - core, rows], core_in.at[k, rows], sibling, 8 * OWN[c])

            return 0

        lax.fori_loop(0, 2, one, 0)
        if not k:

            def block(i, total):
                return total + dbr[pl.ds(pl.multiple_of(8 * OFF[c] + i * 16, 16), 16), :].astype(F32)

            b_down_sum[...] = lax.fori_loop(0, OWN[c] // 2, block, b_down_sum[...])

    def part_rows(k, c, start, count):
        return part.at[k, core, rows_at(8 * OFF[c] + start, count)]

    def half_columns(side):
        return pl.ds(side * WIDE, WIDE)

    def add_core(k, c):
        p = OWN[c]
        arrived("core", k, c)

        def add(start, count):
            accumulate(k, c, start, count, [lambda at, size: core_in[k, rows_at(8 * OFF[c] + start + at, size), :]])

        if (k, c) in SUM_Z:
            for x in range(4):
                start = (2 * x + 1 - zh) * p
                add(start, p)
                send("z", k, c, part_rows(k, c, start, p), z_in.at[k, pl.ds(Z_OFF[k][c] + x * p, p)], across, p)
            for x in range(4):
                add((2 * x + zh) * p, p)
        else:
            add(x_far * 2 * p, 2 * p)
            for side, device in enumerate((right, left)):
                source = part_rows(k, c, x_far * 2 * p + side * p, p)
                send("x1", k, c, source, x1_in.at[k, side, pl.ds(OFF[c], p)], device, p)
            for piece in (x_right, x_left, xi):
                add(piece * 2 * p, 2 * p)

    def add_first(k, c):
        p = OWN[c]
        sides = ((x_right, right), (x_left, left))
        if (k, c) in SUM_Z:
            arrived("z", k, c)

            def add(piece):
                accumulate(
                    k, c, (2 * piece + zh) * p, p, [lambda at, size: z_in[k, rows_at(Z_OFF[k][c] + piece * p + at, size), :]]
                )

            add(x_far)
            far = part_rows(k, c, (2 * x_far + zh) * p, p)
            for side, (_, device) in enumerate(sides):
                target = x1_in.at[k, side, pl.ds(OFF[c], p), half_columns(side)]
                send("x1", k, c, far.at[:, half_columns(side)], target, device, p // 2)
            for piece in (x_right, x_left, xi):
                add(piece)
        else:
            arrived("x1", k, c)
            for side, (piece, device) in enumerate(sides):
                accumulate(
                    k, c, piece * 2 * p + side * p, p, [lambda at, size: x1_in[k, side, rows_at(OFF[c] + at, size), :]]
                )
                source = part_rows(k, c, piece * 2 * p, 2 * p)
                send("x2", k, c, source, x2_in.at[k, side, pl.ds(2 * OFF[c], 2 * p)], device, 2 * p)

    def add_second(k, c):
        p = OWN[c]
        if (k, c) in SUM_Z:
            arrived("x1", k, c)
            for side, (piece, device) in enumerate(((x_right, right), (x_left, left))):
                columns = half_columns(side)
                accumulate(
                    k, c, (2 * piece + zh) * p, p, [lambda at, size: x1_in[k, side, rows_at(OFF[c] + at, size), columns]], columns
                )
                source = part_rows(k, c, (2 * piece + zh) * p, p)
                send("x2", k, c, source, x2_in.at[k, side, pl.ds(2 * OFF[c], p)], device, p)
            return
        arrived("x2", k, c)

        def add(sub):
            start = sub * p
            accumulate(
                k, c, xi * 2 * p + start, p,
                [lambda at, size, side=side: x2_in[k, side, rows_at(2 * OFF[c] + start + at, size), :] for side in range(2)],
            )

        add(1 - zh)
        source = part_rows(k, c, xi * 2 * p + (1 - zh) * p, p)
        send("z", k, c, source, z_in.at[k, pl.ds(Z_OFF[k][c], p)], across, p)
        add(zh)

    def activate(_, c):
        p = OWN[c]
        mine = (2 * xi + zh) * p
        for k in range(2):
            arrived("x2" if (k, c) in SUM_Z else "z", k, c)
        bias = b_up_ref[pl.ds(pl.multiple_of(core * HALF, HALF), HALF)].reshape(1, HALF)

        def total(k, at):
            value = part[k, core, rows_at(8 * OFF[c] + mine + at, 16), :].astype(F32)
            if (k, c) in SUM_Z:
                for side in range(2):
                    value = value + x2_in[k, side, rows_at(2 * OFF[c] + at, 16), :].astype(F32)
                return value
            return value + z_in[k, rows_at(Z_OFF[k][c] + at, 16), :].astype(F32)

        def block(i, _):
            at = i * 16
            rows = rows_at(8 * OFF[c] + mine + at, 16)
            h = total(1, at) + bias
            square = h * h
            t = jnp.tanh(K0 * (h + K1 * (square * h)))
            full[0, core, rows, :] = (0.5 * h * (1.0 + t)).astype(BF16)
            slope = 0.5 * (1.0 + t) + 0.5 * h * (1.0 - t * t) * (K0 * (1.0 + 3.0 * K1 * square))
            full[1, core, rows, :] = (total(0, at) * slope).astype(BF16)
            return 0

        lax.fori_loop(0, p // 16, block, 0)
        for k in (1, 0):
            place = full.at[k, core, rows_at(8 * OFF[c] + mine, p)]
            for device in (right, left) if (k, c) in GATHER_X else (across,):
                send("ga", k, c, place, place, device, p)

    def full_rows(k, c, start, count):
        return full.at[k, core, rows_at(8 * OFF[c] + start, count)]

    def pass_on(kind, k, c, start, count, device):
        place = full_rows(k, c, start, count)
        send(kind, k, c, place, place, device, count)

    def gather_first(k, c):
        p = OWN[c]
        arrived("ga", k, c)
        if (k, c) in GATHER_X:
            for side, (piece, device) in enumerate(((x_left, right), (x_right, left))):
                place = full_rows(k, c, (2 * piece + zh) * p, p).at[:, half_columns(side)]
                send("gf", k, c, place, place, device, p // 2)
        else:
            for device in (right, left):
                pass_on("gx", k, c, xi * 2 * p, 2 * p, device)
            pass_on("gc", k, c, xi * 2 * p, 2 * p, sibling)

    def gather_second(k, c):
        p = OWN[c]
        if (k, c) in GATHER_X:
            arrived("gf", k, c)
            for x in range(4):
                pass_on("gx", k, c, (2 * x + zh) * p, p, across)
            for x in range(4):
                pass_on("gc", k, c, (2 * x + zh) * p, p, sibling)
        else:
            arrived("gx", k, c)
            for side, (piece, device) in enumerate(((x_left, right), (x_right, left))):
                pass_on("gf", k, c, piece * 2 * p + side * p, p, device)
            for piece in (x_left, x_right):
                pass_on("gc", k, c, piece * 2 * p, 2 * p, sibling)

    def gather_third(k, c):
        p = OWN[c]
        if (k, c) in GATHER_X:
            arrived("gx", k, c)
            for x in range(4):
                pass_on("gc", k, c, (2 * x + 1 - zh) * p, p, sibling)
        else:
            arrived("gf", k, c)
            pass_on("gc", k, c, x_far * 2 * p, 2 * p, sibling)

    def multiply_back(k, c):
        p = OWN[c]
        arrived("gc", k, c)
        rows = pl.ds(8 * OFF[c], 8 * p)

        def tile(j, _):
            at = pl.ds(pl.multiple_of(j * 256, 256), 256)
            if k:
                value = transposed_dot(full[1, 0, rows, :], w_up[0, at, :])
                value += transposed_dot(full[1, 1, rows, :], w_up[1, at, :])
            else:
                value = jnp.dot(full[0, 0, rows, :], w_down[0, :, at], preferred_element_type=F32)
                value += jnp.dot(full[0, 1, rows, :], w_down[1, :, at], preferred_element_type=F32)
            t_out[k, rows, at] = value.astype(BF16)
            return 0

        lax.fori_loop(0, WIDE // 256, tile, 0)
        if k:
            for half in range(2):
                store(full.at[1, half, rows], gh_hbm.at[rows, pl.ds(half * HALF, HALF)])
            store(nrm.at[rows], nrm_hbm.at[rows])
        if c in R_PAIRS:
            for s, device in enumerate(y_to):
                place = t_out.at[k, rows_at(8 * OFF[c] + (device[1] // 2) * 2 * p, 2 * p)]
                send("ts", k, c, place, t_in.at[k, pl.ds(7 * OFF[c] + s * 2 * p, 2 * p)], device, 2 * p)
        else:
            for s, device in enumerate(t_to):
                place = t_out.at[k, rows_at(8 * OFF[c] + device[1] * p, p)]
                send("ts", k, c, place, t_in.at[k, pl.ds(7 * OFF[c] + s * p, p)], device, p)
        if k:
            for half in range(2):

                def block(i, total):
                    return total + full[1, half, pl.ds(pl.multiple_of(8 * OFF[c] + i * 16, 16), 16), :].astype(F32)

                b_up_sum[half] = lax.fori_loop(0, p // 2, block, b_up_sum[half])

    def halve_tokens(k, c):
        p = OWN[c]
        arrived("ts", k, c)

        def total(sub):
            value = t_out[k, rows_at(8 * OFF[c] + (yi * 2 + sub) * p, p), :].astype(F32)
            for s in range(3):
                value = value + t_in[k, rows_at(7 * OFF[c] + s * 2 * p + sub * p, p), :].astype(F32)
            return value

        place = rows_at(8 * OFF[c] + (yi * 2 + 1 - zl) * p, p)
        t_out[k, place, :] = total(1 - zl).astype(BF16)
        send("tr", k, c, t_out.at[k, place], t_in.at[k, pl.ds(7 * OFF[c] + 6 * p, p)], t_pair, p)
        t_acc[k, OFF[c] : OFF[c] + p, :] = total(zl)

    def finish_tokens(k, c):
        p = OWN[c]
        rows = slice(OFF[c], OFF[c] + p)
        if c in R_PAIRS:
            arrived("tr", k, c)
            value = t_acc[k, rows, :] + t_in[k, 7 * OFF[c] + 6 * p : 7 * OFF[c] + 7 * p, :].astype(F32)
        else:
            arrived("ts", k, c)
            value = t_out[k, rows_at(8 * OFF[c] + tensor * p, p), :].astype(F32)
            for s in range(7):
                value = value + t_in[k, 7 * OFF[c] + s * p : 7 * OFF[c] + (s + 1) * p, :].astype(F32)
        if k:
            grad_normed[rows, :] = value
        else:
            branch_ref[rows, :] = (value + b_down_ref[...].reshape(1, WIDE)).astype(BF16)

    def weight_down(_, half):
        def strip(i, _):
            at = pl.ds(pl.multiple_of(i * STRIP, STRIP), STRIP)
            w_down[half, at, :] = dot_transposed(full[0, half, :, at], dbr[...]).astype(BF16)
            target = gw_down_hbm.at[pl.ds(pl.multiple_of(half * HALF + i * STRIP, STRIP), STRIP)]
            pltpu.make_async_copy(w_down.at[half, at], target, strip_sem.at[half]).start()
            return 0

        lax.fori_loop(0, HALF // STRIP, strip, 0)

    def back_sums(k, c):
        gn, std = grad_normed[...], standard[...]
        scaled = gn * gain_ref[...].reshape(1, WIDE)
        back_stats[0] = columns_to_rows(
            jnp.sum(scaled, axis=1, keepdims=True), jnp.sum(scaled * std, axis=1, keepdims=True)
        )
        send_small(1, back_stats, d_to)
        gb[0, 0:1, :] = jnp.sum(gn * std, axis=0, keepdims=True)
        gb[0, 1:2, :] = jnp.sum(gn, axis=0, keepdims=True)
        gb[0, 2:8, :] = jnp.zeros((6, WIDE), F32)
        send_small(2, gb, t_to)
        for half in range(2):
            grad_b_up_ref[half * HALF : (half + 1) * HALF] = jnp.sum(b_up_sum[half], axis=0)
        grad_b_down_ref[...] = jnp.sum(b_down_sum[...], axis=0)
        store(grad_b_up_ref, grad_b_up_hbm)
        store(grad_b_down_ref, grad_b_down_hbm)

    def grad_inputs(k, c):
        wait_small(small_recv.at[1], back_stats)
        first = functools.reduce(jnp.add, [back_stats[s, 0:1, :] for s in range(16)]) / D
        second = functools.reduce(jnp.add, [back_stats[s, 1:2, :] for s in range(16)]) / D
        first, second = rows_to_columns(first, second)
        scaled = grad_normed[...] * gain_ref[...].reshape(1, WIDE)
        grad_in_ref[...] = (inverse_ref[:, 0:1] * (scaled - first - standard[...] * second)).astype(BF16)
        store(grad_in_ref, grad_in_hbm)
        wait_small(small_recv.at[2], gb)
        both = functools.reduce(jnp.add, [gb[s] for s in range(8)])
        grad_gain_ref[...] = both[0]
        grad_bias_ref[...] = both[1]
        store(grad_gain_ref, grad_gain_hbm)
        store(grad_bias_ref, grad_bias_hbm)

    steps = {
        "TZ": pair_tokens, "TY": gather_tokens, "ST": statistics, "NM": normalise, "M": multiply, "A": add_core,
        "B": add_first, "C": add_second, "G": activate, "E1": gather_first, "E2": gather_second, "E3": gather_third,
        "F": multiply_back, "H1": halve_tokens, "H": finish_tokens, "WD": weight_down,
        "S": back_sums, "Z": grad_inputs,
    }
    b_up_sum[...] = jnp.zeros_like(b_up_sum)
    b_down_sum[...] = jnp.zeros_like(b_down_sum)
    for name, k, c in ORDER:
        steps[name](k, c)
    store(branch_ref, branch_hbm)
    for (kind, k), rows in leaving.items():
        wait_rows(kind, rows, send_sem.at[kinds.index(kind), k])
    for index, buffer in enumerate((stats, back_stats, gb)):
        wait_small(small_send.at[index], buffer)
    for copy in stores:
        copy.wait()
    for half in range(2):
        pltpu.make_async_copy(w_down.at[half], gw_down_hbm.at[pl.ds(half * HALF, HALF)], strip_sem.at[half]).wait()


def last_kernel(
    nrm_hbm, gh_hbm, gw_down_hbm, branch_in, grad_in_in, gain_in, bias_in, b_up_in, b_down_in,
    branch_out, grad_in_out, gw_up_out, b_up_out, gw_down_out, b_down_out, gain_out, bias_out,
    nrm, gh, gw_up, gw_down, branch, grad_in, gain, bias, b_up, b_down, in_sem, out_sem,
):
    strips, parts = 2 * HALF // STRIP, 4

    def columns(i):
        return pl.ds(i * STRIP, STRIP)

    ins, outs = [], []

    def fetch(source, target):
        copy = pltpu.make_async_copy(source, target, in_sem.at[len(ins)])
        copy.start()
        ins.append(copy)
        return copy

    def put(source, target):
        copy = pltpu.make_async_copy(source, target, out_sem.at[len(outs)])
        copy.start()
        outs.append(copy)

    first = fetch(nrm_hbm, nrm)
    strip_in = [fetch(gh_hbm.at[:, columns(i)], gh.at[i]) for i in range(strips)]
    rows = [pl.ds(i * (2 * HALF // parts), 2 * HALF // parts) for i in range(parts)]
    passing = [(fetch(gw_down_hbm.at[r], gw_down.at[r]), gw_down.at[r], gw_down_out.at[r]) for r in rows]
    for source, held, target in (
        (branch_in, branch, branch_out), (grad_in_in, grad_in, grad_in_out), (gain_in, gain, gain_out),
        (bias_in, bias, bias_out), (b_up_in, b_up, b_up_out), (b_down_in, b_down, b_down_out),
    ):
        passing.append((fetch(source, held), held, target))
    first.wait()
    for i in range(strips):
        strip_in[i].wait()
        gw_up[i] = dot_transposed(nrm[...], gh[i]).astype(BF16)
        put(gw_up.at[i], gw_up_out.at[:, columns(i)])
        if i >= 2:
            for copy, held, target in passing[(i - 2) * 3 : (i - 1) * 3]:
                copy.wait()
                put(held, target)
    for copy in outs:
        copy.wait()


def on_device(inputs, norm_gain, norm_bias, w_up, b_up, w_down, b_down, d_branch):
    hbm = pl.BlockSpec(memory_space=pl.ANY)
    shape = jax.ShapeDtypeStruct

    dma = pltpu.SemaphoreType.DMA

    branch, grad_in, grad_gain, grad_bias, grad_b_up, grad_b_down, grad_w_down, gh, nrm = pl.pallas_call(
        kernel,
        out_shape=(
            shape((128, WIDE), BF16), shape((128, WIDE), BF16), shape((WIDE,), F32), shape((WIDE,), F32), shape((2 * HALF,), F32),
            shape((WIDE,), F32), shape((2 * HALF, WIDE), BF16), shape((TOKENS, 2 * HALF), BF16), shape((TOKENS, WIDE), BF16),
        ),
        in_specs=[hbm] * 8,
        out_specs=(hbm,) * 9,
        scratch_shapes=[
            pltpu.VMEM((128, WIDE), BF16),
            pltpu.VMEM((WIDE,), F32), pltpu.VMEM((WIDE,), F32), pltpu.VMEM((2 * HALF,), F32), pltpu.VMEM((WIDE,), F32),
            pltpu.VMEM((128, WIDE), BF16), pltpu.VMEM((128, WIDE), BF16),
            pltpu.VMEM((WIDE,), F32), pltpu.VMEM((WIDE,), F32), pltpu.VMEM((2 * HALF,), F32), pltpu.VMEM((WIDE,), F32),
            pltpu.VMEM((2, WIDE, HALF), BF16),
            pltpu.VMEM((2, HALF, WIDE), BF16),
            pltpu.VMEM((TOKENS, WIDE), BF16),
            pltpu.VMEM((TOKENS, WIDE), BF16),
            pltpu.VMEM((2, 2, TOKENS, HALF), BF16),
            pltpu.VMEM((2, TOKENS, HALF), BF16),
            pltpu.VMEM((2, 2, 128, HALF), BF16),
            pltpu.VMEM((2, 2, 256, HALF), BF16),
            pltpu.VMEM((2, max(sum(rows) for rows in Z_ROWS), HALF), BF16),
            pltpu.VMEM((2, 2, TOKENS, HALF), BF16),
            pltpu.VMEM((2, TOKENS, WIDE), BF16),
            pltpu.VMEM((2, 7 * 128, WIDE), BF16),
            pltpu.VMEM((2, 128, WIDE), F32),
            pltpu.VMEM((128, WIDE), F32),
            pltpu.VMEM((128, WIDE), F32),
            pltpu.VMEM((128, 128), F32),
            pltpu.VMEM((16, 8, 128), F32),
            pltpu.VMEM((16, 8, 128), F32),
            pltpu.VMEM((8, 8, WIDE), F32),
            pltpu.VMEM((2, 16, HALF), F32),
            pltpu.VMEM((16, WIDE), F32),
            dma((CHUNKS + 8,)), dma((6 + 3 * CHUNKS,)), dma((2,)), dma((12, 2)), dma((12, 2, CHUNKS)), dma((3,)), dma((3,)),
        ],
        compiler_params=pltpu.CompilerParams(collective_id=0, has_side_effects=True, vmem_limit_bytes=63 * 2**20),
    )(inputs, norm_gain, norm_bias, b_up, b_down, d_branch, w_up, w_down.reshape(2, HALF, WIDE))
    return pl.pallas_call(
        last_kernel,
        out_shape=(
            shape((128, WIDE), BF16), shape((128, WIDE), BF16), shape((WIDE, 2 * HALF), BF16), shape((2 * HALF,), F32),
            shape((2 * HALF, WIDE), BF16), shape((WIDE,), F32), shape((WIDE,), F32), shape((WIDE,), F32),
        ),
        in_specs=[hbm] * 9,
        out_specs=(hbm,) * 8,
        scratch_shapes=[
            pltpu.VMEM((TOKENS, WIDE), BF16),
            pltpu.VMEM((6, TOKENS, STRIP), BF16),
            pltpu.VMEM((6, WIDE, STRIP), BF16),
            pltpu.VMEM((2 * HALF, WIDE), BF16),
            pltpu.VMEM((128, WIDE), BF16), pltpu.VMEM((128, WIDE), BF16),
            pltpu.VMEM((WIDE,), F32), pltpu.VMEM((WIDE,), F32), pltpu.VMEM((2 * HALF,), F32), pltpu.VMEM((WIDE,), F32),
            dma((17,)), dma((16,)),
        ],
        compiler_params=pltpu.CompilerParams(vmem_limit_bytes=63 * 2**20),
    )(nrm, gh, grad_w_down, branch, grad_in, grad_gain, grad_bias, grad_b_up, grad_b_down)


def solution(mesh):
    placed = (
        P("tensor", "dp"), P("dp"), P("dp"), P("dp", "tensor"), P("tensor"), P("tensor", "dp"), P("dp"), P("tensor", "dp"),
    )
    return jax.shard_map(
        on_device,
        mesh=mesh,
        in_specs=placed,
        out_specs=(
            P("tensor", "dp"), P("tensor", "dp"), P("dp", "tensor"), P("tensor"), P("tensor", "dp"), P("dp"), P("dp"), P("dp"),
        ),
        check_vma=False,
    )
```

```python
import functools

import jax
import jax.numpy as jnp
from jax import lax
from jax.experimental import pallas as pl
from jax.experimental.pallas import tpu as pltpu
from jax.sharding import PartitionSpec as P

MESH = pl.DeviceIdType.MESH
F32, BF16 = jnp.float32, jnp.bfloat16

D = 12288
WIDE = 768
HALF = 1536
TOKENS = 1024
STRIP = 512
K0 = 0.7978845608028654
K1 = 0.044715

OWN = (32, 32, 16, 16, 16, 16)
CHUNKS = len(OWN)
OFF = tuple(sum(OWN[:c]) for c in range(CHUNKS))
SUM_Z = ((0, 3), (0, 5), (1, 3), (1, 4), (1, 5))
GATHER_X = ((0, 0), (0, 2), (1, 3), (1, 5))
T_PAIRS = (1, 2, 3, 4, 5)
R_PAIRS = (0, 2)
Z_ROWS = tuple(tuple((4 if (k, c) in SUM_Z else 1) * OWN[c] for c in range(CHUNKS)) for k in range(2))
Z_OFF = tuple(tuple(sum(rows[:c]) for c in range(CHUNKS)) for rows in Z_ROWS)

ORDER = (
    ("TZ", 0, 3), ("TZ", 0, 2), ("TY", 0, 0), ("ST", 0, 0), ("TZ", 0, 1), ("TY", 0, 2), ("TY", 0, 3), ("NM", 0, 0),
    ("TZ", 1, 3), ("TZ", 0, 5), ("TY", 1, 0), ("TZ", 1, 2), ("M", 0, 0), ("TZ", 1, 5), ("TZ", 1, 4), ("TZ", 1, 1),
    ("TY", 1, 3), ("A", 0, 0), ("M", 0, 2), ("M", 0, 3), ("A", 0, 2), ("TY", 1, 2), ("TZ", 0, 4), ("B", 0, 0),
    ("A", 0, 3), ("TY", 0, 5), ("TY", 0, 1), ("M", 1, 0), ("M", 1, 3), ("A", 1, 0), ("TY", 1, 5), ("B", 0, 2),
    ("M", 1, 2), ("A", 1, 3), ("TY", 1, 4), ("TY", 1, 1), ("A", 1, 2), ("B", 0, 3), ("M", 0, 5), ("B", 1, 0),
    ("A", 0, 5), ("TY", 0, 4), ("M", 0, 1), ("B", 1, 3), ("A", 0, 1), ("B", 1, 2), ("C", 0, 0), ("M", 1, 4),
    ("M", 1, 5), ("C", 1, 0), ("C", 0, 3), ("A", 1, 4), ("B", 0, 1), ("M", 1, 1), ("A", 1, 5), ("G", 0, 0),
    ("M", 0, 4), ("A", 1, 1), ("C", 1, 3), ("C", 0, 1), ("E1", 0, 0), ("A", 0, 4), ("B", 0, 5), ("B", 1, 5),
    ("C", 1, 2), ("C", 0, 2), ("B", 1, 1), ("E2", 0, 0), ("C", 0, 5), ("E1", 1, 0), ("C", 1, 5), ("B", 0, 4),
    ("C", 1, 1), ("B", 1, 4), ("G", 0, 2), ("G", 0, 3), ("G", 0, 5), ("C", 0, 4), ("C", 1, 4), ("E3", 0, 0),
    ("E1", 0, 2), ("E2", 1, 0), ("G", 0, 1), ("E1", 1, 2), ("E1", 1, 3), ("E1", 0, 5), ("E2", 0, 2), ("E1", 1, 5),
    ("F", 0, 0), ("E3", 1, 0), ("E2", 1, 2), ("E1", 1, 1), ("G", 0, 4), ("E2", 1, 3), ("F", 1, 0), ("E2", 0, 5),
    ("E3", 0, 2), ("E3", 1, 2), ("E1", 1, 4), ("E1", 0, 4), ("E2", 1, 5), ("F", 0, 2), ("E2", 1, 1), ("F", 1, 2),
    ("E3", 0, 5), ("H1", 0, 0), ("E3", 1, 3), ("F", 0, 5), ("E2", 1, 4), ("E1", 0, 3), ("F", 1, 3), ("H1", 0, 2),
    ("E3", 1, 5), ("E3", 1, 1), ("E1", 0, 1), ("E2", 0, 4), ("H1", 1, 0), ("F", 1, 5), ("H1", 1, 2), ("F", 1, 1),
    ("H", 1, 3), ("E3", 1, 4), ("H", 0, 5), ("E2", 0, 3), ("H", 1, 0), ("E2", 0, 1), ("H", 0, 0), ("F", 1, 4),
    ("E3", 0, 3), ("H", 1, 2), ("E3", 0, 4), ("F", 0, 3), ("H", 0, 2), ("H", 1, 5), ("E3", 0, 1), ("F", 0, 4),
    ("H", 1, 1), ("F", 0, 1), ("H", 1, 4), ("S", 0, 0), ("WD", 0, 1), ("WD", 0, 0), ("Z", 0, 0), ("H", 0, 4),
    ("H", 0, 3), ("H", 0, 1),
)


def transposed_dot(left, right):
    return lax.dot_general(left, right, (((1,), (1,)), ((), ())), preferred_element_type=F32)


def dot_transposed(left, right):
    return lax.dot_general(left, right, (((0,), (0,)), ((), ())), preferred_element_type=F32)


def columns_to_rows(first, second):
    lane = lax.broadcasted_iota(jnp.int32, (128, 128), 1)
    return jnp.where(lane == 0, first, jnp.where(lane == 1, second, 0.0)).T[0:8, :]


def rows_to_columns(first, second):
    row = lax.broadcasted_iota(jnp.int32, (128, 128), 0)
    both = jnp.where(row == 0, first, jnp.where(row == 1, second, 0.0)).T
    return both[:, 0:1], both[:, 1:2]


def kernel(
    x_hbm, gain_hbm, bias_hbm, b_up_hbm, b_down_hbm, d_hbm, w_up_hbm, w_down_hbm,
    branch_hbm, grad_in_hbm, grad_gain_hbm, grad_bias_hbm, grad_b_up_hbm, grad_b_down_hbm, gw_down_hbm, gh_hbm, nrm_hbm,
    x_ref, gain_ref, bias_ref, b_up_ref, b_down_ref,
    branch_ref, grad_in_ref, grad_gain_ref, grad_bias_ref, grad_b_up_ref, grad_b_down_ref,
    w_up, w_down, dbr, nrm, part, core_in, x1_in, x2_in, z_in, full, t_out, t_in, t_acc,
    standard, grad_normed, inverse_ref, stats, back_stats, gb, b_up_sum, b_down_sum,
    load_sem, store_sem, strip_sem, send_sem, recv_sem, small_send, small_recv,
):
    dp, tensor = lax.axis_index("dp"), lax.axis_index("tensor")
    xi, zh, core = dp // 4, (dp // 2) % 2, dp % 2
    yi, zl = tensor // 2, tensor % 2
    x_right, x_left, x_far = (xi + 1) % 4, (xi + 3) % 4, (xi + 2) % 4
    right = (x_right * 4 + zh * 2 + core, tensor)
    left = (x_left * 4 + zh * 2 + core, tensor)
    across = (xi * 4 + (1 - zh) * 2 + core, tensor)
    sibling = (xi * 4 + zh * 2 + (1 - core), tensor)
    t_pair = (dp, yi * 2 + (1 - zl))
    y_to = [(dp, ((yi + dy) % 4) * 2 + zl) for dy in (1, 2, 3)]
    t_to = y_to + [t_pair] + [(dp, ((yi + dy) % 4) * 2 + (1 - zl)) for dy in (1, 2, 3)]
    d_to = []
    for dx in range(4):
        for mz in range(2):
            for mc in range(2):
                if dx or mz or mc:
                    d_to.append((((xi + dx) % 4) * 4 + (1 - zh if mz else zh) * 2 + (1 - core if mc else core), tensor))

    barrier = pltpu.get_barrier_semaphore()
    for device in t_to + d_to:
        pl.semaphore_signal(barrier, inc=1, device_id=device, device_id_type=MESH)

    def rows_at(at, count):
        return pl.ds(pl.multiple_of(at, 16), count)

    pairs = [(d_hbm.at[pl.ds(OFF[c], OWN[c])], dbr.at[rows_at(8 * OFF[c] + tensor * OWN[c], OWN[c])]) for c in range(CHUNKS)]
    pairs += [(x_hbm, x_ref), (gain_hbm, gain_ref), (bias_hbm, bias_ref), (b_up_hbm, b_up_ref), (b_down_hbm, b_down_ref)]
    pairs += [(w_down_hbm, w_down)] + [(w_up_hbm.at[:, pl.ds(h * HALF, HALF)], w_up.at[h]) for h in range(2)]
    loads = [pltpu.make_async_copy(source, target, load_sem.at[i]) for i, (source, target) in enumerate(pairs)]
    for copy in loads:
        copy.start()
    loads = {"d": loads[:CHUNKS], "x": loads[CHUNKS : CHUNKS + 5], 0: loads[CHUNKS + 5 : CHUNKS + 6], 1: loads[CHUNKS + 6 :]}

    def loaded(name):
        for copy in loads.pop(name, ()):
            copy.wait()

    loaded("d")
    pl.semaphore_wait(barrier, len(t_to) + len(d_to))

    kinds = ("t", "tz", "core", "x1", "x2", "z", "ga", "gx", "gf", "gc", "ts", "tr")
    narrow = ("t", "tz", "ts", "tr")
    arriving, leaving = {}, {}

    def send(kind, k, c, source, target, device, rows):
        pltpu.make_async_remote_copy(
            src_ref=source, dst_ref=target, send_sem=send_sem.at[kinds.index(kind), k],
            recv_sem=recv_sem.at[kinds.index(kind), k, c], device_id=device, device_id_type=MESH,
        ).start()
        arriving[kind, k, c] = arriving.get((kind, k, c), 0) + rows
        leaving[kind, k] = leaving.get((kind, k), 0) + rows

    def wait_rows(kind, rows, semaphore):
        place = nrm.at[pl.ds(0, rows)] if kind in narrow else full.at[0, 0, pl.ds(0, rows)]
        pltpu.make_async_copy(place, place, semaphore).wait()

    def arrived(kind, k, c):
        wait_rows(kind, arriving.pop((kind, k, c)), recv_sem.at[kinds.index(kind), k, c])

    def send_small(index, buffer, devices):
        for s, device in enumerate(devices):
            pltpu.make_async_remote_copy(
                src_ref=buffer.at[0], dst_ref=buffer.at[s + 1], send_sem=small_send.at[index],
                recv_sem=small_recv.at[index], device_id=device, device_id_type=MESH,
            ).start()

    def wait_small(semaphore, buffer):
        place = buffer.at[pl.ds(1, buffer.shape[0] - 1)]
        pltpu.make_async_copy(place, place, semaphore).wait()

    stores = []

    def store(source, target):
        copy = pltpu.make_async_copy(source, target, store_sem.at[len(stores)])
        copy.start()
        stores.append(copy)

    tokens = (dbr, nrm)

    def pair_tokens(k, c):
        place = tokens[k].at[rows_at(8 * OFF[c] + tensor * OWN[c], OWN[c])]
        send("tz", k, c, place, place, t_pair, OWN[c])

    def gather_tokens(k, c):
        p = OWN[c]
        if c in T_PAIRS:
            arrived("tz", k, c)
            place = tokens[k].at[rows_at(8 * OFF[c] + yi * 2 * p, 2 * p)]
            for device in y_to:
                send("t", k, c, place, place, device, 2 * p)
        else:
            place = tokens[k].at[rows_at(8 * OFF[c] + tensor * p, p)]
            for device in t_to:
                send("t", k, c, place, place, device, p)

    def statistics(k, c):
        loaded("x")
        widened = x_ref[...].astype(F32)
        total = jnp.sum(widened, axis=1, keepdims=True)
        off = widened - total / WIDE
        stats[0] = columns_to_rows(total, jnp.sum(off * off, axis=1, keepdims=True))
        send_small(0, stats, d_to)

    def normalise(k, c):
        wait_small(small_recv.at[0], stats)
        sums = [stats[s, 0:1, :] for s in range(16)]
        mean = functools.reduce(jnp.add, sums) / D
        spread = jnp.zeros_like(mean)
        for s in range(16):
            apart = sums[s] / WIDE - mean
            spread = spread + (stats[s, 1:2, :] + WIDE * (apart * apart))
        mean, inverse = rows_to_columns(mean, lax.rsqrt(spread / D + 1e-05))
        inverse_ref[...] = jnp.broadcast_to(inverse, (128, 128))
        gain, bias = gain_ref[...].reshape(1, WIDE), bias_ref[...].reshape(1, WIDE)
        for c in range(CHUNKS):
            rows = slice(OFF[c], OFF[c] + OWN[c])
            std = (x_ref[rows, :].astype(F32) - mean[rows]) * inverse[rows]
            standard[rows, :] = std
            nrm[rows_at(8 * OFF[c] + tensor * OWN[c], OWN[c]), :] = (std * gain + bias).astype(BF16)

    def accumulate(k, c, start, count, others, columns=slice(None)):
        size = 32 if count % 32 == 0 else 16

        def block(i, _):
            at = i * size
            rows = rows_at(8 * OFF[c] + start + at, size)
            value = part[k, core, rows, columns].astype(F32)
            for load in others:
                value = value + load(at, size).astype(F32)
            part[k, core, rows, columns] = value.astype(BF16)
            return 0

        if count == size:
            block(0, 0)
        else:
            lax.fori_loop(0, count // size, block, 0)

    def multiply(k, c):
        loaded(k)
        arrived("t", k, c)
        rows = pl.ds(8 * OFF[c], 8 * OWN[c])

        def one(step, _):
            half = (1 - core) * (1 - step) + core * step
            if k:
                value = jnp.dot(nrm[rows, :], w_up[half], preferred_element_type=F32)
            else:
                value = transposed_dot(dbr[rows, :], w_down[half])
            part[k, half, rows, :] = value.astype(BF16)

            @pl.when(step == 0)
            def _():
                send("core", k, c, part.at[k, 1 - core, rows], core_in.at[k, rows], sibling, 8 * OWN[c])

            return 0

        lax.fori_loop(0, 2, one, 0)
        if not k:

            def block(i, total):
                return total + dbr[pl.ds(pl.multiple_of(8 * OFF[c] + i * 16, 16), 16), :].astype(F32)

            b_down_sum[...] = lax.fori_loop(0, OWN[c] // 2, block, b_down_sum[...])

    def part_rows(k, c, start, count):
        return part.at[k, core, rows_at(8 * OFF[c] + start, count)]

    def half_columns(side):
        return pl.ds(side * WIDE, WIDE)

    def add_core(k, c):
        p = OWN[c]
        arrived("core", k, c)

        def add(start, count):
            accumulate(k, c, start, count, [lambda at, size: core_in[k, rows_at(8 * OFF[c] + start + at, size), :]])

        if (k, c) in SUM_Z:
            for x in range(4):
                start = (2 * x + 1 - zh) * p
                add(start, p)
                send("z", k, c, part_rows(k, c, start, p), z_in.at[k, pl.ds(Z_OFF[k][c] + x * p, p)], across, p)
            for x in range(4):
                add((2 * x + zh) * p, p)
        else:
            add(x_far * 2 * p, 2 * p)
            for side, device in enumerate((right, left)):
                source = part_rows(k, c, x_far * 2 * p + side * p, p)
                send("x1", k, c, source, x1_in.at[k, side, pl.ds(OFF[c], p)], device, p)
            for piece in (x_right, x_left, xi):
                add(piece * 2 * p, 2 * p)

    def add_first(k, c):
        p = OWN[c]
        sides = ((x_right, right), (x_left, left))
        if (k, c) in SUM_Z:
            arrived("z", k, c)

            def add(piece):
                accumulate(
                    k, c, (2 * piece + zh) * p, p, [lambda at, size: z_in[k, rows_at(Z_OFF[k][c] + piece * p + at, size), :]]
                )

            add(x_far)
            far = part_rows(k, c, (2 * x_far + zh) * p, p)
            for side, (_, device) in enumerate(sides):
                target = x1_in.at[k, side, pl.ds(OFF[c], p), half_columns(side)]
                send("x1", k, c, far.at[:, half_columns(side)], target, device, p // 2)
            for piece in (x_right, x_left, xi):
                add(piece)
        else:
            arrived("x1", k, c)
            for side, (piece, device) in enumerate(sides):
                accumulate(
                    k, c, piece * 2 * p + side * p, p, [lambda at, size: x1_in[k, side, rows_at(OFF[c] + at, size), :]]
                )
                source = part_rows(k, c, piece * 2 * p, 2 * p)
                send("x2", k, c, source, x2_in.at[k, side, pl.ds(2 * OFF[c], 2 * p)], device, 2 * p)

    def add_second(k, c):
        p = OWN[c]
        if (k, c) in SUM_Z:
            arrived("x1", k, c)
            for side, (piece, device) in enumerate(((x_right, right), (x_left, left))):
                columns = half_columns(side)
                accumulate(
                    k, c, (2 * piece + zh) * p, p, [lambda at, size: x1_in[k, side, rows_at(OFF[c] + at, size), columns]], columns
                )
                source = part_rows(k, c, (2 * piece + zh) * p, p)
                send("x2", k, c, source, x2_in.at[k, side, pl.ds(2 * OFF[c], p)], device, p)
            return
        arrived("x2", k, c)

        def add(sub):
            start = sub * p
            accumulate(
                k, c, xi * 2 * p + start, p,
                [lambda at, size, side=side: x2_in[k, side, rows_at(2 * OFF[c] + start + at, size), :] for side in range(2)],
            )

        add(1 - zh)
        source = part_rows(k, c, xi * 2 * p + (1 - zh) * p, p)
        send("z", k, c, source, z_in.at[k, pl.ds(Z_OFF[k][c], p)], across, p)
        add(zh)

    def activate(_, c):
        p = OWN[c]
        mine = (2 * xi + zh) * p
        for k in range(2):
            arrived("x2" if (k, c) in SUM_Z else "z", k, c)
        bias = b_up_ref[pl.ds(pl.multiple_of(core * HALF, HALF), HALF)].reshape(1, HALF)

        def total(k, at):
            value = part[k, core, rows_at(8 * OFF[c] + mine + at, 16), :].astype(F32)
            if (k, c) in SUM_Z:
                for side in range(2):
                    value = value + x2_in[k, side, rows_at(2 * OFF[c] + at, 16), :].astype(F32)
                return value
            return value + z_in[k, rows_at(Z_OFF[k][c] + at, 16), :].astype(F32)

        def block(i, _):
            at = i * 16
            rows = rows_at(8 * OFF[c] + mine + at, 16)
            h = total(1, at) + bias
            square = h * h
            t = jnp.tanh(K0 * (h + K1 * (square * h)))
            full[0, core, rows, :] = (0.5 * h * (1.0 + t)).astype(BF16)
            slope = 0.5 * (1.0 + t) + 0.5 * h * (1.0 - t * t) * (K0 * (1.0 + 3.0 * K1 * square))
            full[1, core, rows, :] = (total(0, at) * slope).astype(BF16)
            return 0

        lax.fori_loop(0, p // 16, block, 0)
        for k in (1, 0):
            place = full.at[k, core, rows_at(8 * OFF[c] + mine, p)]
            for device in (right, left) if (k, c) in GATHER_X else (across,):
                send("ga", k, c, place, place, device, p)

    def full_rows(k, c, start, count):
        return full.at[k, core, rows_at(8 * OFF[c] + start, count)]

    def pass_on(kind, k, c, start, count, device):
        place = full_rows(k, c, start, count)
        send(kind, k, c, place, place, device, count)

    def gather_first(k, c):
        p = OWN[c]
        arrived("ga", k, c)
        if (k, c) in GATHER_X:
            for side, (piece, device) in enumerate(((x_left, right), (x_right, left))):
                place = full_rows(k, c, (2 * piece + zh) * p, p).at[:, half_columns(side)]
                send("gf", k, c, place, place, device, p // 2)
        else:
            for device in (right, left):
                pass_on("gx", k, c, xi * 2 * p, 2 * p, device)
            pass_on("gc", k, c, xi * 2 * p, 2 * p, sibling)

    def gather_second(k, c):
        p = OWN[c]
        if (k, c) in GATHER_X:
            arrived("gf", k, c)
            for x in range(4):
                pass_on("gx", k, c, (2 * x + zh) * p, p, across)
            for x in range(4):
                pass_on("gc", k, c, (2 * x + zh) * p, p, sibling)
        else:
            arrived("gx", k, c)
            for side, (piece, device) in enumerate(((x_left, right), (x_right, left))):
                pass_on("gf", k, c, piece * 2 * p + side * p, p, device)
            for piece in (x_left, x_right):
                pass_on("gc", k, c, piece * 2 * p, 2 * p, sibling)

    def gather_third(k, c):
        p = OWN[c]
        if (k, c) in GATHER_X:
            arrived("gx", k, c)
            for x in range(4):
                pass_on("gc", k, c, (2 * x + 1 - zh) * p, p, sibling)
        else:
            arrived("gf", k, c)
            pass_on("gc", k, c, x_far * 2 * p, 2 * p, sibling)

    def multiply_back(k, c):
        p = OWN[c]
        arrived("gc", k, c)
        rows = pl.ds(8 * OFF[c], 8 * p)

        def tile(j, _):
            at = pl.ds(pl.multiple_of(j * 256, 256), 256)
            if k:
                value = transposed_dot(full[1, 0, rows, :], w_up[0, at, :])
                value += transposed_dot(full[1, 1, rows, :], w_up[1, at, :])
            else:
                value = jnp.dot(full[0, 0, rows, :], w_down[0, :, at], preferred_element_type=F32)
                value += jnp.dot(full[0, 1, rows, :], w_down[1, :, at], preferred_element_type=F32)
            t_out[k, rows, at] = value.astype(BF16)
            return 0

        lax.fori_loop(0, WIDE // 256, tile, 0)
        if k:
            for half in range(2):
                store(full.at[1, half, rows], gh_hbm.at[rows, pl.ds(half * HALF, HALF)])
            store(nrm.at[rows], nrm_hbm.at[rows])
        if c in R_PAIRS:
            for s, device in enumerate(y_to):
                place = t_out.at[k, rows_at(8 * OFF[c] + (device[1] // 2) * 2 * p, 2 * p)]
                send("ts", k, c, place, t_in.at[k, pl.ds(7 * OFF[c] + s * 2 * p, 2 * p)], device, 2 * p)
        else:
            for s, device in enumerate(t_to):
                place = t_out.at[k, rows_at(8 * OFF[c] + device[1] * p, p)]
                send("ts", k, c, place, t_in.at[k, pl.ds(7 * OFF[c] + s * p, p)], device, p)
        if k:
            for half in range(2):

                def block(i, total):
                    return total + full[1, half, pl.ds(pl.multiple_of(8 * OFF[c] + i * 16, 16), 16), :].astype(F32)

                b_up_sum[half] = lax.fori_loop(0, p // 2, block, b_up_sum[half])

    def halve_tokens(k, c):
        p = OWN[c]
        arrived("ts", k, c)

        def total(sub):
            value = t_out[k, rows_at(8 * OFF[c] + (yi * 2 + sub) * p, p), :].astype(F32)
            for s in range(3):
                value = value + t_in[k, rows_at(7 * OFF[c] + s * 2 * p + sub * p, p), :].astype(F32)
            return value

        place = rows_at(8 * OFF[c] + (yi * 2 + 1 - zl) * p, p)
        t_out[k, place, :] = total(1 - zl).astype(BF16)
        send("tr", k, c, t_out.at[k, place], t_in.at[k, pl.ds(7 * OFF[c] + 6 * p, p)], t_pair, p)
        t_acc[k, OFF[c] : OFF[c] + p, :] = total(zl)

    def finish_tokens(k, c):
        p = OWN[c]
        rows = slice(OFF[c], OFF[c] + p)
        if c in R_PAIRS:
            arrived("tr", k, c)
            value = t_acc[k, rows, :] + t_in[k, 7 * OFF[c] + 6 * p : 7 * OFF[c] + 7 * p, :].astype(F32)
        else:
            arrived("ts", k, c)
            value = t_out[k, rows_at(8 * OFF[c] + tensor * p, p), :].astype(F32)
            for s in range(7):
                value = value + t_in[k, 7 * OFF[c] + s * p : 7 * OFF[c] + (s + 1) * p, :].astype(F32)
        if k:
            grad_normed[rows, :] = value
        else:
            branch_ref[rows, :] = (value + b_down_ref[...].reshape(1, WIDE)).astype(BF16)

    def weight_down(_, half):
        def strip(i, _):
            at = pl.ds(pl.multiple_of(i * STRIP, STRIP), STRIP)
            w_down[half, at, :] = dot_transposed(full[0, half, :, at], dbr[...]).astype(BF16)
            target = gw_down_hbm.at[pl.ds(pl.multiple_of(half * HALF + i * STRIP, STRIP), STRIP)]
            pltpu.make_async_copy(w_down.at[half, at], target, strip_sem.at[half]).start()
            return 0

        lax.fori_loop(0, HALF // STRIP, strip, 0)

    def back_sums(k, c):
        gn, std = grad_normed[...], standard[...]
        scaled = gn * gain_ref[...].reshape(1, WIDE)
        back_stats[0] = columns_to_rows(
            jnp.sum(scaled, axis=1, keepdims=True), jnp.sum(scaled * std, axis=1, keepdims=True)
        )
        send_small(1, back_stats, d_to)
        gb[0, 0:1, :] = jnp.sum(gn * std, axis=0, keepdims=True)
        gb[0, 1:2, :] = jnp.sum(gn, axis=0, keepdims=True)
        gb[0, 2:8, :] = jnp.zeros((6, WIDE), F32)
        send_small(2, gb, t_to)
        for half in range(2):
            grad_b_up_ref[half * HALF : (half + 1) * HALF] = jnp.sum(b_up_sum[half], axis=0)
        grad_b_down_ref[...] = jnp.sum(b_down_sum[...], axis=0)
        store(grad_b_up_ref, grad_b_up_hbm)
        store(grad_b_down_ref, grad_b_down_hbm)

    def grad_inputs(k, c):
        wait_small(small_recv.at[1], back_stats)
        first = functools.reduce(jnp.add, [back_stats[s, 0:1, :] for s in range(16)]) / D
        second = functools.reduce(jnp.add, [back_stats[s, 1:2, :] for s in range(16)]) / D
        first, second = rows_to_columns(first, second)
        scaled = grad_normed[...] * gain_ref[...].reshape(1, WIDE)
        grad_in_ref[...] = (inverse_ref[:, 0:1] * (scaled - first - standard[...] * second)).astype(BF16)
        store(grad_in_ref, grad_in_hbm)
        wait_small(small_recv.at[2], gb)
        both = functools.reduce(jnp.add, [gb[s] for s in range(8)])
        grad_gain_ref[...] = both[0]
        grad_bias_ref[...] = both[1]
        store(grad_gain_ref, grad_gain_hbm)
        store(grad_bias_ref, grad_bias_hbm)

    steps = {
        "TZ": pair_tokens, "TY": gather_tokens, "ST": statistics, "NM": normalise, "M": multiply, "A": add_core,
        "B": add_first, "C": add_second, "G": activate, "E1": gather_first, "E2": gather_second, "E3": gather_third,
        "F": multiply_back, "H1": halve_tokens, "H": finish_tokens, "WD": weight_down,
        "S": back_sums, "Z": grad_inputs,
    }
    b_up_sum[...] = jnp.zeros_like(b_up_sum)
    b_down_sum[...] = jnp.zeros_like(b_down_sum)
    for name, k, c in ORDER:
        steps[name](k, c)
    store(branch_ref, branch_hbm)
    for (kind, k), rows in leaving.items():
        wait_rows(kind, rows, send_sem.at[kinds.index(kind), k])
    for index, buffer in enumerate((stats, back_stats, gb)):
        wait_small(small_send.at[index], buffer)
    for copy in stores:
        copy.wait()
    for half in range(2):
        pltpu.make_async_copy(w_down.at[half], gw_down_hbm.at[pl.ds(half * HALF, HALF)], strip_sem.at[half]).wait()


def last_kernel(
    nrm_hbm, gh_hbm, gw_down_hbm, branch_in, grad_in_in, gain_in, bias_in, b_up_in, b_down_in,
    branch_out, grad_in_out, gw_up_out, b_up_out, gw_down_out, b_down_out, gain_out, bias_out,
    nrm, gh, gw_up, gw_down, branch, grad_in, gain, bias, b_up, b_down, in_sem, out_sem,
):
    strips, parts = 2 * HALF // STRIP, 4

    def columns(i):
        return pl.ds(i * STRIP, STRIP)

    ins, outs = [], []

    def fetch(source, target):
        copy = pltpu.make_async_copy(source, target, in_sem.at[len(ins)])
        copy.start()
        ins.append(copy)
        return copy

    def put(source, target):
        copy = pltpu.make_async_copy(source, target, out_sem.at[len(outs)])
        copy.start()
        outs.append(copy)

    first = fetch(nrm_hbm, nrm)
    strip_in = [fetch(gh_hbm.at[:, columns(i)], gh.at[i]) for i in range(strips)]
    rows = [pl.ds(i * (2 * HALF // parts), 2 * HALF // parts) for i in range(parts)]
    passing = [(fetch(gw_down_hbm.at[r], gw_down.at[r]), gw_down.at[r], gw_down_out.at[r]) for r in rows]
    for source, held, target in (
        (branch_in, branch, branch_out), (grad_in_in, grad_in, grad_in_out), (gain_in, gain, gain_out),
        (bias_in, bias, bias_out), (b_up_in, b_up, b_up_out), (b_down_in, b_down, b_down_out),
    ):
        passing.append((fetch(source, held), held, target))
    first.wait()
    for i in range(strips):
        strip_in[i].wait()
        gw_up[i] = dot_transposed(nrm[...], gh[i]).astype(BF16)
        put(gw_up.at[i], gw_up_out.at[:, columns(i)])
        if i >= 2:
            for copy, held, target in passing[(i - 2) * 3 : (i - 1) * 3]:
                copy.wait()
                put(held, target)
    for copy in outs:
        copy.wait()


def on_device(inputs, norm_gain, norm_bias, w_up, b_up, w_down, b_down, d_branch):
    hbm = pl.BlockSpec(memory_space=pl.ANY)
    shape = jax.ShapeDtypeStruct

    dma = pltpu.SemaphoreType.DMA

    branch, grad_in, grad_gain, grad_bias, grad_b_up, grad_b_down, grad_w_down, gh, nrm = pl.pallas_call(
        kernel,
        out_shape=(
            shape((128, WIDE), BF16), shape((128, WIDE), BF16), shape((WIDE,), F32), shape((WIDE,), F32), shape((2 * HALF,), F32),
            shape((WIDE,), F32), shape((2 * HALF, WIDE), BF16), shape((TOKENS, 2 * HALF), BF16), shape((TOKENS, WIDE), BF16),
        ),
        in_specs=[hbm] * 8,
        out_specs=(hbm,) * 9,
        scratch_shapes=[
            pltpu.VMEM((128, WIDE), BF16),
            pltpu.VMEM((WIDE,), F32), pltpu.VMEM((WIDE,), F32), pltpu.VMEM((2 * HALF,), F32), pltpu.VMEM((WIDE,), F32),
            pltpu.VMEM((128, WIDE), BF16), pltpu.VMEM((128, WIDE), BF16),
            pltpu.VMEM((WIDE,), F32), pltpu.VMEM((WIDE,), F32), pltpu.VMEM((2 * HALF,), F32), pltpu.VMEM((WIDE,), F32),
            pltpu.VMEM((2, WIDE, HALF), BF16),
            pltpu.VMEM((2, HALF, WIDE), BF16),
            pltpu.VMEM((TOKENS, WIDE), BF16),
            pltpu.VMEM((TOKENS, WIDE), BF16),
            pltpu.VMEM((2, 2, TOKENS, HALF), BF16),
            pltpu.VMEM((2, TOKENS, HALF), BF16),
            pltpu.VMEM((2, 2, 128, HALF), BF16),
            pltpu.VMEM((2, 2, 256, HALF), BF16),
            pltpu.VMEM((2, max(sum(rows) for rows in Z_ROWS), HALF), BF16),
            pltpu.VMEM((2, 2, TOKENS, HALF), BF16),
            pltpu.VMEM((2, TOKENS, WIDE), BF16),
            pltpu.VMEM((2, 7 * 128, WIDE), BF16),
            pltpu.VMEM((2, 128, WIDE), F32),
            pltpu.VMEM((128, WIDE), F32),
            pltpu.VMEM((128, WIDE), F32),
            pltpu.VMEM((128, 128), F32),
            pltpu.VMEM((16, 8, 128), F32),
            pltpu.VMEM((16, 8, 128), F32),
            pltpu.VMEM((8, 8, WIDE), F32),
            pltpu.VMEM((2, 16, HALF), F32),
            pltpu.VMEM((16, WIDE), F32),
            dma((CHUNKS + 8,)), dma((6 + 3 * CHUNKS,)), dma((2,)), dma((12, 2)), dma((12, 2, CHUNKS)), dma((3,)), dma((3,)),
        ],
        compiler_params=pltpu.CompilerParams(collective_id=0, has_side_effects=True, vmem_limit_bytes=63 * 2**20),
    )(inputs, norm_gain, norm_bias, b_up, b_down, d_branch, w_up, w_down.reshape(2, HALF, WIDE))
    return pl.pallas_call(
        last_kernel,
        out_shape=(
            shape((128, WIDE), BF16), shape((128, WIDE), BF16), shape((WIDE, 2 * HALF), BF16), shape((2 * HALF,), F32),
            shape((2 * HALF, WIDE), BF16), shape((WIDE,), F32), shape((WIDE,), F32), shape((WIDE,), F32),
        ),
        in_specs=[hbm] * 9,
        out_specs=(hbm,) * 8,
        scratch_shapes=[
            pltpu.VMEM((TOKENS, WIDE), BF16),
            pltpu.VMEM((6, TOKENS, STRIP), BF16),
            pltpu.VMEM((6, WIDE, STRIP), BF16),
            pltpu.VMEM((2 * HALF, WIDE), BF16),
            pltpu.VMEM((128, WIDE), BF16), pltpu.VMEM((128, WIDE), BF16),
            pltpu.VMEM((WIDE,), F32), pltpu.VMEM((WIDE,), F32), pltpu.VMEM((2 * HALF,), F32), pltpu.VMEM((WIDE,), F32),
            dma((17,)), dma((16,)),
        ],
        compiler_params=pltpu.CompilerParams(vmem_limit_bytes=63 * 2**20),
    )(nrm, gh, grad_w_down, branch, grad_in, grad_gain, grad_bias, grad_b_up, grad_b_down)


def solution(mesh):
    placed = (
        P("tensor", "dp"), P("dp"), P("dp"), P("dp", "tensor"), P("tensor"), P("tensor", "dp"), P("dp"), P("tensor", "dp"),
    )
    return jax.shard_map(
        on_device,
        mesh=mesh,
        in_specs=placed,
        out_specs=(
            P("tensor", "dp"), P("tensor", "dp"), P("dp", "tensor"), P("tensor"), P("tensor", "dp"), P("dp"), P("dp"), P("dp"),
        ),
        check_vma=False,
    )
```
